32 devices in a mesh: az: 4 (over y, x), rad: 8 (over z, core).
Axes of the slice: x: 2, y: 2, z: 4, core: 2. Of those that a mesh axis runs over, the one named last changes fastest.
Arguments:
- field: bfloat16 [256, 4, 1024, 128], P('az', None, 'rad'), may hold values from -6 to 6
- shell_counts: int32 [8], replicated, may hold values from 1 to 128, 512 in all
- op_index: int32 [129], replicated, may hold values from 0 to 1
- radial_ops: bfloat16 [2, 512, 512], replicated, may hold values from -0.25 to 0.25
Outputs:
- result: bfloat16 [256, 4, 128, 512], P('az', None, 'rad')
The draws below stay inside these ranges and needn't reach their ends.
Inputs may be any that keep to these rules, and one draw needn't show every extreme that they name: Rad index j holds shell_counts[j] radial cells in its first slots, shells in order from the axis outward; its other slots hold no data; the counts sum to 512 and the largest equals 128. op_index[m] names the radial operator of azimuthal mode number m.
All inputs are finite; a program needn't handle non-finite values.
Results may differ from the reference program's by a relative error of at most 0.0059.
Values may be sent and summed in bfloat16 or wider, within the bound.
A program may use at most 192 MiB of HBM per device.

```python
import math
import jax
import jax.numpy as jnp
import numpy as np
from jax import lax

A = 256
R = 512
F = 4
NOPS = 2
X = 128
RCAP = 128
SLOTS = 1024
MODES = 129
N_RAD = 8


def touch_ends(array, rng, smallest, high):
    index_at = [jax.random.randint(jax.random.fold_in(rng, axis), (), 0, length) for axis, length in enumerate(array.shape)]
    longest = array.shape.index(max(array.shape))
    beside = index_at[:longest] + [(index_at[longest] + 1) % array.shape[longest]] + index_at[longest + 1:]
    return array.at[tuple(index_at)].set(smallest).at[tuple(beside)].set(high)


def block_scale(rng, shape, split, least, high):
    loudness = 1.0
    for position, parts in split:
        heights = jax.random.uniform(jax.random.fold_in(jax.random.fold_in(rng, 6), position), (parts,), jnp.float32, least / len(split), high / len(split))
        loudness = loudness * jnp.repeat(jnp.exp(heights), shape[position] // parts).reshape((-1,) + (1,) * (len(shape) - 1 - position))
    return loudness


def profile(count, total, most, slope):
    portions = [(1 << 20) // math.isqrt(rank ** slope) + 1 for rank in range(2, count + 1)]
    surplus, given = total - most - (count - 1), [1] * (count - 1)
    while surplus > 0:
        movable = [i for i in range(count - 1) if given[i] < most]
        whole, budget = sum([portions[i] for i in movable]), surplus
        for i in movable:
            addition = min(most - given[i], max(1, budget * portions[i] // whole), surplus)
            given[i] = given[i] + addition
            surplus = surplus - addition
    return np.array([most] + given)


def ragged_sizes(stream_key, amount, total, bound, lean):
    if amount == 2:
        one = jax.random.randint(stream_key, (), max(1, total - bound), min(bound, total - 1) + 1)
        return jnp.stack([one, total - one])
    tallies = jnp.asarray(profile(amount, total, bound, lean), jnp.int32)
    twos = (amount - 1) // 2
    donor, sink = tallies[1:1 + 2 * twos:2], tallies[2:2 + 2 * twos:2]
    margin = jnp.minimum(donor - 1, bound - sink)
    moved = jax.random.randint(jax.random.fold_in(stream_key, 1), (twos,), 0, 1 << 20) % (margin + 1)
    tallies = tallies.at[1:1 + 2 * twos:2].set(donor - moved).at[2:2 + 2 * twos:2].set(sink + moved)
    return tallies[jax.random.permutation(jax.random.fold_in(stream_key, 2), amount)]


def centred(own_key, dims, deviation, limit, cuts=(), kind=jnp.bfloat16):
    array = deviation * jax.random.normal(own_key, dims, jnp.float32)
    if cuts:
        array = array * block_scale(own_key, dims, cuts, -0.22, 0.18)
    return jnp.clip(array, -limit, limit).astype(kind)


def setup_inputs(seed: int = 0) -> dict:
    seeds = jax.random.split(jax.random.key(seed), 5)
    return {
        "field": centred(seeds[0], (A, F, SLOTS, X), 1.0, 6.0, ((0, 4), (2, 8))),
        "shell_counts": ragged_sizes(seeds[1], N_RAD, R, RCAP, 1).astype(jnp.int32),
        "op_index": touch_ends(jax.random.randint(seeds[2], (MODES,), 0, NOPS), jax.random.fold_in(seeds[2], 1), 0, NOPS - 1).astype(jnp.int32),
        "radial_ops": centred(seeds[3], (NOPS, R, R), R ** -0.5, 0.25),
    }


def make_table(length):
    index = jnp.arange(length, dtype=jnp.int32)
    product = index[:, None] * index[None, :] % length
    angle = product.astype(jnp.float32) * (2.0 * math.pi / length)
    return ((jnp.cos(angle) + jnp.sin(angle)) * (1.0 / math.sqrt(length))).astype(jnp.bfloat16)

def slot_index(counts, capacity, radial):
    counts = counts.astype(jnp.int32)
    starts = (jnp.cumsum(counts) - counts).astype(jnp.int32)
    rows = jnp.arange(radial, dtype=jnp.int32)
    owner = (lax.optimization_barrier(jnp.sum((starts[None, :] <= rows[:, None]).astype(jnp.int32), axis=1)) - 1).astype(jnp.int32)
    return (owner * capacity + rows - jnp.take(starts, owner)).astype(jnp.int32)

def reference(field, shell_counts, op_index, radial_ops):
    row_slot = slot_index(shell_counts, RCAP, R)
    cas_table = make_table(A)
    spectra_list = []
    for which in range(F):
        packed = jnp.take(field[:, which], row_slot, axis=1)
        flat = jnp.dot(cas_table, packed.reshape(A, R * X), preferred_element_type=jnp.float32)
        spectra_list.append(flat.astype(jnp.bfloat16).reshape(A, R, X))
    spectra = jnp.stack(spectra_list, axis=1)
    comps = jnp.arange(A, dtype=jnp.int32)
    operator = jnp.take(op_index, jnp.minimum(comps, A - comps)).astype(jnp.int32)

    def apply_one(pair):
        chosen, values = pair
        matrix = radial_ops[chosen].astype(jnp.float32)
        mapped = jnp.einsum('rs,fsx->fxr', matrix, values.astype(jnp.float32), precision=lax.Precision.HIGHEST)
        return mapped.astype(jnp.bfloat16)
    return lax.map(apply_one, (operator, spectra))
```

```python
import functools
import math

import jax
import jax.numpy as jnp
from jax import lax
from jax.experimental import pallas as pl
from jax.experimental.pallas import tpu as pltpu
from jax.sharding import PartitionSpec as P

MESH = pl.DeviceIdType.MESH
VMEM_LIMIT = 48 << 20
AHEAD = 2


def make_table(length):
    index = jnp.arange(length, dtype=jnp.int32)
    product = index[:, None] * index[None, :] % length
    angle = product.astype(jnp.float32) * (2.0 * math.pi / length)
    return ((jnp.cos(angle) + jnp.sin(angle)) * (1.0 / math.sqrt(length))).astype(jnp.bfloat16)


def slot_index(counts, capacity, radial):
    starts = jnp.cumsum(counts) - counts
    rows = jnp.arange(radial, dtype=jnp.int32)
    owner = jnp.sum((starts[None, :] <= rows[:, None]).astype(jnp.int32), axis=1) - 1
    return owner * capacity + rows - jnp.take(starts, owner)


def to_planes(values):
    return lax.all_to_all(values, "az", split_axis=3, concat_axis=0, tiled=True)


def to_modes(values):
    return lax.all_to_all(values, "az", split_axis=0, concat_axis=3, tiled=True)


def regroup_shells(values):
    return lax.all_to_all(values, "rad", split_axis=3, concat_axis=2, tiled=True)


def transform(cas_table, values):
    shape = values.shape
    flat = jnp.dot(cas_table, values.reshape(shape[0], -1), preferred_element_type=jnp.float32)
    return flat.astype(jnp.bfloat16).reshape(shape)


def plain_path(field, row_slot, cas_table, chosen_ids, radial_ops):
    chosen = jnp.take(radial_ops, chosen_ids, axis=0)
    gathered = to_planes(field)
    spectra = transform(cas_table, gathered)
    returned = to_modes(spectra)
    slab_data = regroup_shells(returned)
    packed = jnp.take(slab_data, row_slot, axis=2)
    result = jnp.einsum("crs,cfsx->cfxr", chosen, packed, preferred_element_type=jnp.float32)
    return result.astype(jnp.bfloat16)


def lay_out_kernel(field_ref, out_ref):
    turned = jnp.swapaxes(field_ref[:, 0], 1, 2)
    by_cell = jnp.swapaxes(turned, 0, 1)
    slabs, _, slab, block, slots = out_ref.shape
    out_ref[:, 0] = by_cell.reshape(slabs, slab, block, slots)


def lay_out(field, n_rad):
    planes, fields, slots, cells = field.shape
    slab = cells // n_rad
    block = 16
    return pl.pallas_call(
        lay_out_kernel,
        grid=(fields, planes // block),
        in_specs=[pl.BlockSpec((block, 1, slots, cells), lambda f, a: (a, f, 0, 0))],
        out_specs=pl.BlockSpec((n_rad, 1, slab, block, slots), lambda f, a: (0, f, 0, a, 0)),
        out_shape=jax.ShapeDtypeStruct((n_rad, fields, slab, planes, slots), field.dtype),
        compiler_params=pltpu.CompilerParams(vmem_limit_bytes=VMEM_LIMIT),
    )(field)


def exchange_kernel(n_az, n_rad, cells_ref, pack_ref, cas_ref, out_ref, shells, packed, planes_in,
                    spectra, rad_send, rad_recv, az_send, az_recv, back_send, back_recv, local_sem):
    az, rad = lax.axis_index("az"), lax.axis_index("rad")
    _, fields, slab, planes, slots = shells.shape
    block = packed.shape[4]

    barrier = pltpu.get_barrier_semaphore()
    for step in range(1, n_rad):
        pl.semaphore_signal(barrier, inc=1, device_id=(az, lax.rem(rad + step, n_rad)), device_id_type=MESH)
    for step in range(1, n_az):
        pl.semaphore_signal(barrier, inc=1, device_id=(lax.rem(az + step, n_az), rad), device_id_type=MESH)
    pl.semaphore_wait(barrier, n_rad + n_az - 2)

    def rad_copy(f, step):
        other = lax.rem(rad + step, n_rad)
        return pltpu.make_async_remote_copy(
            src_ref=cells_ref.at[other, f], dst_ref=shells.at[rad, f],
            send_sem=rad_send.at[f, step], recv_sem=rad_recv.at[f, step],
            device_id=(az, other), device_id_type=MESH)

    def az_copy(f, step):
        other = lax.rem(az + step, n_az)
        return pltpu.make_async_remote_copy(
            src_ref=packed.at[f, other], dst_ref=planes_in.at[f, az],
            send_sem=az_send.at[f, step], recv_sem=az_recv.at[f, step],
            device_id=(other, rad), device_id_type=MESH)

    def back_copy(f, step):
        other = lax.rem(az + step, n_az)
        return pltpu.make_async_remote_copy(
            src_ref=spectra.at[f, other], dst_ref=out_ref.at[f, az],
            send_sem=back_send.at[f, step], recv_sem=back_recv.at[f, step],
            device_id=(other, rad), device_id_type=MESH)

    def own_shells(f):
        return pltpu.make_async_copy(cells_ref.at[rad, f], shells.at[rad, f], local_sem.at[f, 0])

    def own_planes(f):
        return pltpu.make_async_copy(packed.at[f, az], planes_in.at[f, az], local_sem.at[f, 1])

    def own_spectra(f):
        return pltpu.make_async_copy(spectra.at[f, az], out_ref.at[f, az], local_sem.at[f, 2])

    rad_steps = sorted(range(1, n_rad), key=lambda step: abs(step - n_rad // 2))
    az_steps = range(1, n_az)

    def start_rad(f):
        for step in rad_steps:
            rad_copy(f, step).start()
        own_shells(f).start()

    for f in range(min(AHEAD, fields)):
        start_rad(f)

    for f in range(fields):
        for step in rad_steps:
            rad_copy(f, step).wait_recv()
        own_shells(f).wait()
        if f + AHEAD < fields:
            start_rad(f + AHEAD)

        @pl.loop(0, slab // 4)
        def _(part):
            here = pl.ds(part * 4, 4)
            rows = [shells[j, f, here].reshape(4 * planes, slots) for j in range(n_rad)]
            dense = jnp.dot(jnp.concatenate(rows, axis=1), pack_ref[...], preferred_element_type=jnp.float32)
            dense = dense.astype(jnp.bfloat16)
            for k in range(n_az):
                packed[f, k, here] = dense[:, k * block:(k + 1) * block].reshape(4, planes, block)

        for step in az_steps:
            az_copy(f, step).start()
        own_planes(f).start()
        for step in az_steps:
            az_copy(f, step).wait_recv()
        own_planes(f).wait()

        @pl.loop(0, slab // 2)
        def _(part):
            both = [planes_in[f, :, part * 2 + x].reshape(n_az * planes, block) for x in range(2)]
            modes = jnp.dot(cas_ref[...], jnp.concatenate(both, axis=1), preferred_element_type=jnp.float32)
            modes = modes.astype(jnp.bfloat16)
            for x in range(2):
                for k in range(n_az):
                    spectra[f, k, part * 2 + x] = modes[k * planes:(k + 1) * planes, x * block:(x + 1) * block]

        for step in az_steps:
            back_copy(f, step).start()
        own_spectra(f).start()

    for f in range(fields):
        for step in az_steps:
            back_copy(f, step).wait_recv()
        own_spectra(f).wait()
        for step in rad_steps:
            rad_copy(f, step).wait_send()
        for step in az_steps:
            az_copy(f, step).wait_send()
            back_copy(f, step).wait_send()


def exchange(cells, pack, cas_table, n_az, n_rad):
    _, fields, slab, planes, slots = cells.shape
    radial = pack.shape[1]
    block = radial // n_az
    kind = cells.dtype
    dma = pltpu.SemaphoreType.DMA
    return pl.pallas_call(
        functools.partial(exchange_kernel, n_az, n_rad),
        in_specs=[
            pl.BlockSpec(memory_space=pl.ANY),
            pl.BlockSpec(memory_space=pltpu.VMEM),
            pl.BlockSpec(memory_space=pltpu.VMEM),
        ],
        out_specs=pl.BlockSpec(memory_space=pl.ANY),
        out_shape=jax.ShapeDtypeStruct((fields, n_az, slab, planes, block), kind),
        scratch_shapes=[
            pltpu.VMEM((n_rad, fields, slab, planes, slots), kind),
            pltpu.VMEM((fields, n_az, slab, planes, block), kind),
            pltpu.VMEM((fields, n_az, slab, planes, block), kind),
            pltpu.VMEM((fields, n_az, slab, planes, block), kind),
            dma((fields, n_rad)), dma((fields, n_rad)),
            dma((fields, n_az)), dma((fields, n_az)),
            dma((fields, n_az)), dma((fields, n_az)),
            dma((fields, 3)),
        ],
        compiler_params=pltpu.CompilerParams(
            collective_id=0, has_side_effects=True, vmem_limit_bytes=VMEM_LIMIT),
    )(cells, pack, cas_table)


def radial_kernel(modes_ref, ops_ref, which_ref, out_ref):
    _, blocks, slab, comps, block = modes_ref.shape
    radial = blocks * block
    rows = [modes_ref[0, b].reshape(slab * comps, block) for b in range(blocks)]
    rows = jnp.concatenate(rows, axis=1)
    mapped = []
    for n in range(2):
        whole = lax.dot_general(rows, ops_ref[n], (((1,), (1,)), ((), ())), preferred_element_type=jnp.float32)
        mapped.append(jnp.swapaxes(whole.reshape(slab, comps, radial), 0, 1))
    out_ref[:, 0] = jnp.where(which_ref[...] > 0, mapped[1], mapped[0]).astype(out_ref.dtype)


def apply_radial(modes, radial_ops, chosen_ids):
    fields, blocks, slab, comps, block = modes.shape
    radial = blocks * block
    part = 16
    which = jnp.broadcast_to(chosen_ids[:, None, None], (comps, 1, radial))
    return pl.pallas_call(
        radial_kernel,
        grid=(fields, comps // part),
        in_specs=[
            pl.BlockSpec((1, blocks, slab, part, block), lambda f, c: (f, 0, 0, c, 0)),
            pl.BlockSpec((2, radial, radial), lambda f, c: (0, 0, 0)),
            pl.BlockSpec((part, 1, radial), lambda f, c: (c, 0, 0)),
        ],
        out_specs=pl.BlockSpec((part, 1, slab, radial), lambda f, c: (c, f, 0, 0)),
        out_shape=jax.ShapeDtypeStruct((comps, fields, slab, radial), modes.dtype),
        compiler_params=pltpu.CompilerParams(vmem_limit_bytes=VMEM_LIMIT),
    )(modes, radial_ops, which)


def per_device(field, shell_counts, op_index, radial_ops):
    planes, fields, slots, cells = field.shape
    n_az, n_rad = lax.axis_size("az"), lax.axis_size("rad")
    comps_all = planes * n_az
    radial = radial_ops.shape[1]
    row_slot = slot_index(shell_counts, slots, radial)
    cas_table = make_table(comps_all)
    comp_ids = lax.axis_index("az") * planes + jnp.arange(planes, dtype=jnp.int32)
    mode_ids = jnp.minimum(comp_ids, comps_all - comp_ids)
    chosen_ids = jnp.take(op_index, mode_ids)
    slab = cells // n_rad
    if slots % 128 or cells % 128 or slab % 16 or planes % 16 or radial % (128 * n_az):
        return plain_path(field, row_slot, cas_table, chosen_ids, radial_ops)
    pack = (jnp.arange(n_rad * slots, dtype=jnp.int32)[:, None] == row_slot[None, :]).astype(field.dtype)
    modes = exchange(lay_out(field, n_rad), pack, cas_table, n_az, n_rad)
    return apply_radial(modes, radial_ops, chosen_ids)


def solution(mesh):
    return jax.shard_map(
        per_device,
        mesh=mesh,
        in_specs=(P("az", None, "rad", None), P(), P(), P()),
        out_specs=P("az", None, "rad", None),
        check_vma=False,
    )
```

```python
import functools
import math

import jax
import jax.numpy as jnp
from jax import lax
from jax.experimental import pallas as pl
from jax.experimental.pallas import tpu as pltpu
from jax.sharding import PartitionSpec as P

MESH = pl.DeviceIdType.MESH
VMEM_LIMIT = 56 << 20
PART = 4


def make_table(length):
    index = jnp.arange(length, dtype=jnp.int32)
    product = index[:, None] * index[None, :] % length
    angle = product.astype(jnp.float32) * (2.0 * math.pi / length)
    return ((jnp.cos(angle) + jnp.sin(angle)) * (1.0 / math.sqrt(length))).astype(jnp.bfloat16)


def slot_index(counts, capacity, radial):
    starts = jnp.cumsum(counts) - counts
    rows = jnp.arange(radial, dtype=jnp.int32)
    owner = jnp.sum((starts[None, :] <= rows[:, None]).astype(jnp.int32), axis=1) - 1
    return owner * capacity + rows - jnp.take(starts, owner)


def to_planes(values):
    return lax.all_to_all(values, "az", split_axis=3, concat_axis=0, tiled=True)


def to_modes(values):
    return lax.all_to_all(values, "az", split_axis=0, concat_axis=3, tiled=True)


def regroup_shells(values):
    return lax.all_to_all(values, "rad", split_axis=3, concat_axis=2, tiled=True)


def transform(cas_table, values):
    shape = values.shape
    flat = jnp.dot(cas_table, values.reshape(shape[0], -1), preferred_element_type=jnp.float32)
    return flat.astype(jnp.bfloat16).reshape(shape)


def plain_path(field, row_slot, cas_table, chosen_ids, radial_ops):
    chosen = jnp.take(radial_ops, chosen_ids, axis=0)
    gathered = to_planes(field)
    spectra = transform(cas_table, gathered)
    returned = to_modes(spectra)
    slab_data = regroup_shells(returned)
    packed = jnp.take(slab_data, row_slot, axis=2)
    result = jnp.einsum("crs,cfsx->cfxr", chosen, packed, preferred_element_type=jnp.float32)
    return result.astype(jnp.bfloat16)


def exchange_kernel(n_az, n_rad, field_ref, pack_ref, cas_ref, out_ref, raw, cells, shells, packed,
                    planes_in, spectra, rad_send, rad_recv, az_send, az_recv, back_send, back_recv,
                    own_sem, raw_sem):
    az, rad = lax.axis_index("az"), lax.axis_index("rad")
    _, fields, slab, planes, slots = shells.shape
    block = packed.shape[4]
    parts = slab // PART
    chunks = fields * parts

    def raw_copy(f):
        return pltpu.make_async_copy(field_ref.at[:, f], raw.at[f], raw_sem.at[f])

    for f in range(fields):
        raw_copy(f).start()

    barrier = pltpu.get_barrier_semaphore()
    for step in range(1, n_rad):
        pl.semaphore_signal(barrier, inc=1, device_id=(az, lax.rem(rad + step, n_rad)), device_id_type=MESH)
    for step in range(1, n_az):
        pl.semaphore_signal(barrier, inc=1, device_id=(lax.rem(az + step, n_az), rad), device_id_type=MESH)

    def place(q):
        return q // parts, pl.ds((q % parts) * PART, PART)

    def rad_copy(q, step):
        f, here = place(q)
        other = lax.rem(rad + step, n_rad)
        return pltpu.make_async_remote_copy(
            src_ref=cells.at[other, f, here], dst_ref=shells.at[rad, f, here],
            send_sem=rad_send.at[q, step], recv_sem=rad_recv.at[q, step],
            device_id=(az, other), device_id_type=MESH)

    def az_copy(q, step):
        f, here = place(q)
        other = lax.rem(az + step, n_az)
        return pltpu.make_async_remote_copy(
            src_ref=packed.at[f, other, here], dst_ref=planes_in.at[f, az, here],
            send_sem=az_send.at[q, step], recv_sem=az_recv.at[q, step],
            device_id=(other, rad), device_id_type=MESH)

    def back_copy(q, step):
        f, here = place(q)
        other = lax.rem(az + step, n_az)
        return pltpu.make_async_remote_copy(
            src_ref=spectra.at[f, other, here], dst_ref=out_ref.at[f, az, here],
            send_sem=back_send.at[q, step], recv_sem=back_recv.at[q, step],
            device_id=(other, rad), device_id_type=MESH)

    def own_shells(q):
        f, here = place(q)
        return pltpu.make_async_copy(cells.at[rad, f, here], shells.at[rad, f, here], own_sem.at[q, 0])

    def own_planes(q):
        f, here = place(q)
        return pltpu.make_async_copy(packed.at[f, az, here], planes_in.at[f, az, here], own_sem.at[q, 1])

    def own_spectra(q):
        f, here = place(q)
        return pltpu.make_async_copy(spectra.at[f, az, here], out_ref.at[f, az, here], own_sem.at[q, 2])

    rad_steps = sorted(range(1, n_rad), key=lambda step: abs(step - n_rad // 2))
    az_steps = range(1, n_az)

    def lay_out(f):
        raw_copy(f).wait()

        @pl.loop(0, planes // 16)
        def _(part):
            here = pl.ds(part * 16, 16)
            turned = jnp.swapaxes(raw[f, here], 1, 2)
            by_cell = jnp.swapaxes(turned, 0, 1)
            cells[:, f, :, here, :] = by_cell.reshape(n_rad, slab, 16, slots)

    def start_rad(q):
        for step in rad_steps:
            rad_copy(q, step).start()
        own_shells(q).start()

    def finish(q):
        f, _ = place(q)
        for step in az_steps:
            az_copy(q, step).wait_recv()
        own_planes(q).wait()

        @pl.loop(0, PART // 2)
        def _(pair):
            first = (q % parts) * PART + pair * 2
            both = [planes_in[f, :, first + x].reshape(n_az * planes, block) for x in range(2)]
            modes = jnp.dot(cas_ref[...], jnp.concatenate(both, axis=1), preferred_element_type=jnp.float32)
            modes = modes.astype(jnp.bfloat16)
            for x in range(2):
                for k in range(n_az):
                    spectra[f, k, first + x] = modes[k * planes:(k + 1) * planes, x * block:(x + 1) * block]

        for step in az_steps:
            back_copy(q, step).start()
        own_spectra(q).start()

    lay_out(0)
    pl.semaphore_wait(barrier, n_rad + n_az - 2)
    for q in range(parts):
        start_rad(q)

    @pl.loop(0, chunks)
    def _(q):
        f, here = place(q)

        @pl.when((q % parts == 0) & (f + 1 < fields))
        def _():
            lay_out(f + 1)

        for step in rad_steps:
            rad_copy(q, step).wait_recv()
        own_shells(q).wait()

        @pl.when(q + parts < chunks)
        def _():
            start_rad(q + parts)

        rows = [shells[j, f, here].reshape(PART * planes, slots) for j in range(n_rad)]
        dense = jnp.dot(jnp.concatenate(rows, axis=1), pack_ref[...], preferred_element_type=jnp.float32)
        dense = dense.astype(jnp.bfloat16)
        for k in range(n_az):
            packed[f, k, here] = dense[:, k * block:(k + 1) * block].reshape(PART, planes, block)

        for step in az_steps:
            az_copy(q, step).start()
        own_planes(q).start()

        @pl.when(q > 0)
        def _():
            finish(q - 1)

    finish(chunks - 1)

    @pl.loop(0, chunks)
    def _(q):
        for step in az_steps:
            back_copy(q, step).wait_recv()
        own_spectra(q).wait()
        for step in rad_steps:
            rad_copy(q, step).wait_send()
        for step in az_steps:
            az_copy(q, step).wait_send()
            back_copy(q, step).wait_send()


def exchange(field, pack, cas_table, n_az, n_rad):
    planes, fields, slots, length = field.shape
    slab = length // n_rad
    block = pack.shape[1] // n_az
    chunks = fields * slab // PART
    kind = field.dtype
    dma = pltpu.SemaphoreType.DMA
    return pl.pallas_call(
        functools.partial(exchange_kernel, n_az, n_rad),
        in_specs=[
            pl.BlockSpec(memory_space=pl.ANY),
            pl.BlockSpec(memory_space=pltpu.VMEM),
            pl.BlockSpec(memory_space=pltpu.VMEM),
        ],
        out_specs=pl.BlockSpec(memory_space=pl.ANY),
        out_shape=jax.ShapeDtypeStruct((fields, n_az, slab, planes, block), kind),
        scratch_shapes=[
            pltpu.VMEM((fields, planes, slots, length), kind),
            pltpu.VMEM((n_rad, fields, slab, planes, slots), kind),
            pltpu.VMEM((n_rad, fields, slab, planes, slots), kind),
            pltpu.VMEM((fields, n_az, slab, planes, block), kind),
            pltpu.VMEM((fields, n_az, slab, planes, block), kind),
            pltpu.VMEM((fields, n_az, slab, planes, block), kind),
            dma((chunks, n_rad)), dma((chunks, n_rad)),
            dma((chunks, n_az)), dma((chunks, n_az)),
            dma((chunks, n_az)), dma((chunks, n_az)),
            dma((chunks, 3)), dma((fields,)),
        ],
        compiler_params=pltpu.CompilerParams(
            collective_id=0, has_side_effects=True, vmem_limit_bytes=VMEM_LIMIT),
    )(field, pack, cas_table)


def radial_kernel(modes_ref, ops_ref, which_ref, out_ref):
    _, blocks, slab, comps, block = modes_ref.shape
    radial = blocks * block
    rows = [modes_ref[0, b].reshape(slab * comps, block) for b in range(blocks)]
    rows = jnp.concatenate(rows, axis=1)
    mapped = []
    for n in range(2):
        whole = lax.dot_general(rows, ops_ref[n], (((1,), (1,)), ((), ())), preferred_element_type=jnp.float32)
        mapped.append(whole.reshape(slab, comps, radial))
    picked = jnp.where(which_ref[...] > 0, mapped[1], mapped[0])
    out_ref[:, 0] = jnp.swapaxes(picked, 0, 1).astype(out_ref.dtype)


def apply_radial(modes, radial_ops, chosen_ids):
    fields, blocks, slab, comps, block = modes.shape
    radial = blocks * block
    part = 16
    which = jnp.broadcast_to(chosen_ids[None, :, None], (1, comps, radial))
    return pl.pallas_call(
        radial_kernel,
        grid=(fields, comps // part),
        in_specs=[
            pl.BlockSpec((1, blocks, slab, part, block), lambda f, c: (f, 0, 0, c, 0)),
            pl.BlockSpec((2, radial, radial), lambda f, c: (0, 0, 0)),
            pl.BlockSpec((1, part, radial), lambda f, c: (0, c, 0)),
        ],
        out_specs=pl.BlockSpec((part, 1, slab, radial), lambda f, c: (c, f, 0, 0)),
        out_shape=jax.ShapeDtypeStruct((comps, fields, slab, radial), modes.dtype),
        compiler_params=pltpu.CompilerParams(vmem_limit_bytes=VMEM_LIMIT),
    )(modes, radial_ops, which)


def per_device(field, shell_counts, op_index, radial_ops):
    planes, fields, slots, cells = field.shape
    n_az, n_rad = lax.axis_size("az"), lax.axis_size("rad")
    comps_all = planes * n_az
    radial = radial_ops.shape[1]
    cas_table = make_table(comps_all)
    comp_ids = lax.axis_index("az") * planes + jnp.arange(planes, dtype=jnp.int32)
    mode_ids = jnp.minimum(comp_ids, comps_all - comp_ids)
    slab = cells // n_rad
    if slots % 128 or cells % 128 or slab % 16 or planes % 16 or radial % (128 * n_az):
        row_slot = slot_index(shell_counts, slots, radial)
        return plain_path(field, row_slot, cas_table, jnp.take(op_index, mode_ids), radial_ops)
    shells = jnp.arange(n_rad, dtype=jnp.int32)
    starts = jnp.sum(jnp.where(shells[None, :] < shells[:, None], shell_counts[None, :], 0), axis=1)
    slot = jnp.arange(slots, dtype=jnp.int32)[None, :]
    row_of = jnp.where(slot < shell_counts[:, None], starts[:, None] + slot, -1)
    pack = row_of[:, :, None] == jnp.arange(radial, dtype=jnp.int32)[None, None, :]
    pack = pack.astype(field.dtype).reshape(n_rad * slots, radial)
    numbers = jnp.arange(op_index.shape[0], dtype=jnp.int32)
    chosen_ids = jnp.sum(jnp.where(mode_ids[:, None] == numbers[None, :], op_index[None, :], 0), axis=1)
    modes = exchange(field, pack, cas_table, n_az, n_rad)
    return apply_radial(modes, radial_ops, chosen_ids)


def solution(mesh):
    return jax.shard_map(
        per_device,
        mesh=mesh,
        in_specs=(P("az", None, "rad", None), P(), P(), P()),
        out_specs=P("az", None, "rad", None),
        check_vma=False,
    )
```

```python
import functools
import math

import jax
import jax.numpy as jnp
from jax import lax
from jax.experimental import pallas as pl
from jax.experimental.pallas import tpu as pltpu
from jax.sharding import PartitionSpec as P

MESH = pl.DeviceIdType.MESH
VMEM_LIMIT = 56 << 20
PART = 4
AHEAD = 3


def make_table(length):
    index = jnp.arange(length, dtype=jnp.int32)
    product = index[:, None] * index[None, :] % length
    angle = product.astype(jnp.float32) * (2.0 * math.pi / length)
    return ((jnp.cos(angle) + jnp.sin(angle)) * (1.0 / math.sqrt(length))).astype(jnp.bfloat16)


def slot_index(counts, capacity, radial):
    starts = jnp.cumsum(counts) - counts
    rows = jnp.arange(radial, dtype=jnp.int32)
    owner = jnp.sum((starts[None, :] <= rows[:, None]).astype(jnp.int32), axis=1) - 1
    return owner * capacity + rows - jnp.take(starts, owner)


def to_planes(values):
    return lax.all_to_all(values, "az", split_axis=3, concat_axis=0, tiled=True)


def to_modes(values):
    return lax.all_to_all(values, "az", split_axis=0, concat_axis=3, tiled=True)


def regroup_shells(values):
    return lax.all_to_all(values, "rad", split_axis=3, concat_axis=2, tiled=True)


def transform(cas_table, values):
    shape = values.shape
    flat = jnp.dot(cas_table, values.reshape(shape[0], -1), preferred_element_type=jnp.float32)
    return flat.astype(jnp.bfloat16).reshape(shape)


def plain_path(field, row_slot, cas_table, chosen_ids, radial_ops):
    chosen = jnp.take(radial_ops, chosen_ids, axis=0)
    gathered = to_planes(field)
    spectra = transform(cas_table, gathered)
    returned = to_modes(spectra)
    slab_data = regroup_shells(returned)
    packed = jnp.take(slab_data, row_slot, axis=2)
    result = jnp.einsum("crs,cfsx->cfxr", chosen, packed, preferred_element_type=jnp.float32)
    return result.astype(jnp.bfloat16)


def exchange_kernel(n_az, n_rad, field_ref, pack_ref, cas_ref, out_ref, raw, cells, shells, packed,
                    planes_in, spectra, rad_send, rad_recv, az_send, az_recv, back_send, back_recv,
                    own_sem, raw_sem):
    az, rad = lax.axis_index("az"), lax.axis_index("rad")
    _, fields, slab, planes, slots = shells.shape
    block = packed.shape[4]
    parts = slab // PART
    chunks = fields * parts

    def raw_copy(f):
        return pltpu.make_async_copy(field_ref.at[:, f], raw.at[f], raw_sem.at[f])

    for f in range(fields):
        raw_copy(f).start()

    barrier = pltpu.get_barrier_semaphore()
    for step in range(1, n_rad):
        pl.semaphore_signal(barrier, inc=1, device_id=(az, lax.rem(rad + step, n_rad)), device_id_type=MESH)
    for step in range(1, n_az):
        pl.semaphore_signal(barrier, inc=1, device_id=(lax.rem(az + step, n_az), rad), device_id_type=MESH)

    def place(q):
        return q // parts, pl.ds((q % parts) * PART, PART)

    def rad_copy(q, step):
        f, here = place(q)
        other = lax.rem(rad + step, n_rad)
        return pltpu.make_async_remote_copy(
            src_ref=cells.at[other, f, here], dst_ref=shells.at[rad, f, here],
            send_sem=rad_send.at[q, step], recv_sem=rad_recv.at[q, step],
            device_id=(az, other), device_id_type=MESH)

    def az_copy(q, step):
        f, here = place(q)
        other = lax.rem(az + step, n_az)
        return pltpu.make_async_remote_copy(
            src_ref=packed.at[f, other, here], dst_ref=planes_in.at[f, az, here],
            send_sem=az_send.at[q, step], recv_sem=az_recv.at[q, step],
            device_id=(other, rad), device_id_type=MESH)

    def back_copy(q, step):
        f, here = place(q)
        other = lax.rem(az + step, n_az)
        return pltpu.make_async_remote_copy(
            src_ref=spectra.at[f, other, here], dst_ref=out_ref.at[f, az, here],
            send_sem=back_send.at[q, step], recv_sem=back_recv.at[q, step],
            device_id=(other, rad), device_id_type=MESH)

    def own_shells(q):
        f, here = place(q)
        return pltpu.make_async_copy(cells.at[rad, f, here], shells.at[rad, f, here], own_sem.at[q, 0])

    def own_planes(q):
        f, here = place(q)
        return pltpu.make_async_copy(packed.at[f, az, here], planes_in.at[f, az, here], own_sem.at[q, 1])

    def own_spectra(q):
        f, here = place(q)
        return pltpu.make_async_copy(spectra.at[f, az, here], out_ref.at[f, az, here], own_sem.at[q, 2])

    rad_steps = sorted(range(1, n_rad), key=lambda step: abs(step - n_rad // 2))
    az_steps = range(1, n_az)

    def lay_out(f):
        raw_copy(f).wait()

        @pl.loop(0, planes // 16)
        def _(part):
            here = pl.ds(part * 16, 16)
            turned = jnp.swapaxes(raw[f, here], 1, 2)
            by_cell = jnp.swapaxes(turned, 0, 1)
            cells[:, f, :, here, :] = by_cell.reshape(n_rad, slab, 16, slots)

    def start_rad(q):
        for step in rad_steps:
            rad_copy(q, step).start()
        own_shells(q).start()

    def finish(q):
        f, _ = place(q)
        for step in az_steps:
            az_copy(q, step).wait_recv()
        own_planes(q).wait()

        @pl.loop(0, PART // 2)
        def _(pair):
            first = (q % parts) * PART + pair * 2
            both = [planes_in[f, :, first + x].reshape(n_az * planes, block) for x in range(2)]
            modes = jnp.dot(cas_ref[...], jnp.concatenate(both, axis=1), preferred_element_type=jnp.float32)
            modes = modes.astype(jnp.bfloat16)
            for x in range(2):
                for k in range(n_az):
                    spectra[f, k, first + x] = modes[k * planes:(k + 1) * planes, x * block:(x + 1) * block]

        for step in az_steps:
            back_copy(q, step).start()
        own_spectra(q).start()

    lay_out(0)
    pl.semaphore_wait(barrier, n_rad + n_az - 2)
    for q in range(parts):
        start_rad(q)

    @pl.loop(0, chunks)
    def _(q):
        f, here = place(q)

        @pl.when((q % parts == 0) & (f + 1 < fields))
        def _():
            lay_out(f + 1)

        for step in rad_steps:
            rad_copy(q, step).wait_recv()
        own_shells(q).wait()

        @pl.when(q + parts < chunks)
        def _():
            start_rad(q + parts)

        rows = [shells[j, f, here].reshape(PART * planes, slots) for j in range(n_rad)]
        dense = jnp.dot(jnp.concatenate(rows, axis=1), pack_ref[...], preferred_element_type=jnp.float32)
        dense = dense.astype(jnp.bfloat16)
        for k in range(n_az):
            packed[f, k, here] = dense[:, k * block:(k + 1) * block].reshape(PART, planes, block)

        for step in az_steps:
            az_copy(q, step).start()
        own_planes(q).start()

        @pl.when(q > 0)
        def _():
            finish(q - 1)

    finish(chunks - 1)

    @pl.loop(0, chunks)
    def _(q):
        for step in az_steps:
            back_copy(q, step).wait_recv()
        own_spectra(q).wait()
        for step in rad_steps:
            rad_copy(q, step).wait_send()
        for step in az_steps:
            az_copy(q, step).wait_send()
            back_copy(q, step).wait_send()


def exchange(field, pack, cas_table, n_az, n_rad):
    planes, fields, slots, length = field.shape
    slab = length // n_rad
    block = pack.shape[1] // n_az
    chunks = fields * slab // PART
    kind = field.dtype
    dma = pltpu.SemaphoreType.DMA
    return pl.pallas_call(
        functools.partial(exchange_kernel, n_az, n_rad),
        in_specs=[
            pl.BlockSpec(memory_space=pl.ANY),
            pl.BlockSpec(memory_space=pltpu.VMEM),
            pl.BlockSpec(memory_space=pltpu.VMEM),
        ],
        out_specs=pl.BlockSpec(memory_space=pl.ANY),
        out_shape=jax.ShapeDtypeStruct((fields, n_az, slab, planes, block), kind),
        scratch_shapes=[
            pltpu.VMEM((fields, planes, slots, length), kind),
            pltpu.VMEM((n_rad, fields, slab, planes, slots), kind),
            pltpu.VMEM((n_rad, fields, slab, planes, slots), kind),
            pltpu.VMEM((fields, n_az, slab, planes, block), kind),
            pltpu.VMEM((fields, n_az, slab, planes, block), kind),
            pltpu.VMEM((fields, n_az, slab, planes, block), kind),
            dma((chunks, n_rad)), dma((chunks, n_rad)),
            dma((chunks, n_az)), dma((chunks, n_az)),
            dma((chunks, n_az)), dma((chunks, n_az)),
            dma((chunks, 3)), dma((fields,)),
        ],
        compiler_params=pltpu.CompilerParams(
            collective_id=0, has_side_effects=True, vmem_limit_bytes=VMEM_LIMIT),
    )(field, pack, cas_table)


def chip_kernel(n_az, n_rad, field_ref, near_ref, rest_ref, first_ref, second_ref, cas_ref, out_ref,
                raw, cells, beside, outgoing, shells, packed, planes_in, spectra, pair_send, pair_recv,
                rad_send, rad_recv, az_send, az_recv, back_send, back_recv, own_sem, raw_sem):
    az, rad = lax.axis_index("az"), lax.axis_index("rad")
    chip, core = rad // 2, rad % 2
    _, fields, slab, planes, slots = cells.shape
    block = packed.shape[4]
    half = planes // 2
    parts = slab // PART
    chunks = fields * parts

    def raw_copy(f):
        return pltpu.make_async_copy(field_ref.at[:, f], raw.at[f], raw_sem.at[f])

    for f in range(fields):
        raw_copy(f).start()

    barrier = pltpu.get_barrier_semaphore()
    for step in range(1, n_rad):
        pl.semaphore_signal(barrier, inc=1, device_id=(az, lax.rem(rad + step, n_rad)), device_id_type=MESH)
    for step in range(1, n_az):
        pl.semaphore_signal(barrier, inc=1, device_id=(lax.rem(az + step, n_az), rad), device_id_type=MESH)

    def place(q):
        return q // parts, pl.ds((q % parts) * PART, PART)

    def halves(which):
        return pl.ds(pl.multiple_of(which * half, half), half)

    def pair_copy(q):
        f, here = place(q)
        return pltpu.make_async_remote_copy(
            src_ref=cells.at[:, f, here, halves(1 - core)], dst_ref=beside.at[q],
            send_sem=pair_send.at[q], recv_sem=pair_recv.at[q],
            device_id=(az, chip * 2 + 1 - core), device_id_type=MESH)

    def rad_copy(q, step):
        other = lax.rem(rad + step, n_rad)
        return pltpu.make_async_remote_copy(
            src_ref=outgoing.at[other, q], dst_ref=shells.at[chip, q, :, halves(core)],
            send_sem=rad_send.at[q, step], recv_sem=rad_recv.at[q, step],
            device_id=(az, other), device_id_type=MESH)

    def az_copy(q, step):
        f, here = place(q)
        other = lax.rem(az + step, n_az)
        return pltpu.make_async_remote_copy(
            src_ref=packed.at[f, other, here], dst_ref=planes_in.at[f, az, here],
            send_sem=az_send.at[q, step], recv_sem=az_recv.at[q, step],
            device_id=(other, rad), device_id_type=MESH)

    def back_copy(q, step):
        f, here = place(q)
        other = lax.rem(az + step, n_az)
        return pltpu.make_async_remote_copy(
            src_ref=spectra.at[f, other, here], dst_ref=out_ref.at[f, az, here],
            send_sem=back_send.at[q, step], recv_sem=back_recv.at[q, step],
            device_id=(other, rad), device_id_type=MESH)

    def own_shells(q):
        return pltpu.make_async_copy(
            outgoing.at[rad, q], shells.at[chip, q, :, halves(core)], own_sem.at[q, 0])

    def own_planes(q):
        f, here = place(q)
        return pltpu.make_async_copy(packed.at[f, az, here], planes_in.at[f, az, here], own_sem.at[q, 1])

    def own_spectra(q):
        f, here = place(q)
        return pltpu.make_async_copy(spectra.at[f, az, here], out_ref.at[f, az, here], own_sem.at[q, 2])

    rad_steps = sorted(range(1, n_rad), key=lambda step: abs(step - n_rad // 2))
    az_steps = range(1, n_az)

    def lay_out(f):
        raw_copy(f).wait()

        @pl.loop(0, planes // 16)
        def _(part):
            here = pl.ds(part * 16, 16)
            turned = jnp.swapaxes(raw[f, here], 1, 2)
            by_cell = jnp.swapaxes(turned, 0, 1)
            cells[:, f, :, here, :] = by_cell.reshape(n_rad, slab, 16, slots)

    def start_rad(q):
        f, here = place(q)
        pair_copy(q).wait_recv()

        @pl.loop(0, n_rad // 4)
        def _(group):
            to = pl.ds(group * 4, 4)
            mine = cells[to, f, here, halves(core)].reshape(4 * PART * half, slots)
            both = jnp.concatenate([mine, beside[q, to].reshape(4 * PART * half, slots)], axis=1)
            near = jnp.dot(both, near_ref[...], preferred_element_type=jnp.float32)
            outgoing[to, q, :PART] = near.astype(jnp.bfloat16).reshape(4, PART, half, slots)
            split = both.reshape(4, PART, half, 2 * slots)
            ends = [split[:, :PART // 2], split[:, PART // 2:]]
            ends = [end.reshape(4 * PART // 2 * half, 2 * slots) for end in ends]
            rest = jnp.dot(jnp.concatenate(ends, axis=1), rest_ref[...], preferred_element_type=jnp.float32)
            outgoing[to, q, PART:] = rest.astype(jnp.bfloat16).reshape(4, PART // 2, half, slots)

        for step in rad_steps:
            rad_copy(q, step).start()
        own_shells(q).start()

    def finish(q):
        f, _ = place(q)
        for step in az_steps:
            az_copy(q, step).wait_recv()
        own_planes(q).wait()

        @pl.loop(0, PART // 2)
        def _(pair):
            first = (q % parts) * PART + pair * 2
            both = [planes_in[f, :, first + x].reshape(n_az * planes, block) for x in range(2)]
            modes = jnp.dot(cas_ref[...], jnp.concatenate(both, axis=1), preferred_element_type=jnp.float32)
            modes = modes.astype(jnp.bfloat16)
            for x in range(2):
                for k in range(n_az):
                    spectra[f, k, first + x] = modes[k * planes:(k + 1) * planes, x * block:(x + 1) * block]

        for step in az_steps:
            back_copy(q, step).start()
        own_spectra(q).start()

    lay_out(0)
    pl.semaphore_wait(barrier, n_rad + n_az - 2)
    for q in range(parts):
        pair_copy(q).start()

    @pl.loop(0, AHEAD)
    def _(q):
        start_rad(q)

    @pl.loop(0, chunks)
    def _(q):
        f, here = place(q)

        @pl.when((q % parts == 0) & (f + 1 < fields))
        def _():
            lay_out(f + 1)
            for part in range(parts):
                pair_copy(q + parts + part).start()

        @pl.when(q + AHEAD < chunks)
        def _():
            start_rad(q + AHEAD)

        for step in rad_steps:
            rad_copy(q, step).wait_recv()
        own_shells(q).wait()

        chips = range(n_rad // 2)
        rows = [shells[j, q, :PART].reshape(PART * planes, slots) for j in chips]
        dense = jnp.dot(jnp.concatenate(rows, axis=1), first_ref[...], preferred_element_type=jnp.float32)
        rows = [shells[j, q, PART:].reshape(PART // 2 * planes, slots) for j in chips]
        rows = jnp.concatenate(rows, axis=1)
        rest = [jnp.dot(rows, second_ref[n], preferred_element_type=jnp.float32) for n in range(2)]
        dense = dense + jnp.concatenate(rest, axis=0)
        dense = dense.astype(jnp.bfloat16)
        for k in range(n_az):
            packed[f, k, here] = dense[:, k * block:(k + 1) * block].reshape(PART, planes, block)

        for step in az_steps:
            az_copy(q, step).start()
        own_planes(q).start()

        @pl.when(q > 0)
        def _():
            finish(q - 1)

    finish(chunks - 1)

    @pl.loop(0, chunks)
    def _(q):
        for step in az_steps:
            back_copy(q, step).wait_recv()
        own_spectra(q).wait()
        pair_copy(q).wait_send()
        for step in rad_steps:
            rad_copy(q, step).wait_send()
        for step in az_steps:
            az_copy(q, step).wait_send()
            back_copy(q, step).wait_send()


def exchange_packed(field, shell_counts, starts, radial, cas_table, n_az, n_rad):
    planes, fields, slots, length = field.shape
    slab = length // n_rad
    block = radial // n_az
    chunks = fields * slab // PART
    units = PART + PART // 2
    kind = field.dtype
    dma = pltpu.SemaphoreType.DMA
    rad = lax.axis_index("rad")
    index = jnp.arange(n_rad, dtype=jnp.int32)
    count_of = lambda which: jnp.sum(jnp.where(index == which, shell_counts, 0))
    slot = jnp.arange(slots, dtype=jnp.int32)
    other = rad + 1 - 2 * (rad % 2)
    mine, theirs = count_of(rad), count_of(other)
    spot = jnp.concatenate([
        jnp.where(slot < mine, slot + jnp.where(rad % 2 == 1, theirs, 0), -1),
        jnp.where(slot < theirs, slot + jnp.where(rad % 2 == 1, 0, mine), -1)])
    near = (spot[:, None] == slot[None, :]).astype(kind)
    late = jnp.where((slot < slots // 2)[None, :], spot[:, None] == slots + slot[None, :], False)
    later = jnp.where((slot >= slots // 2)[None, :], spot[:, None] == slots // 2 + slot[None, :], False)
    rest = jnp.concatenate([late, later], axis=0).astype(kind)
    totals = shell_counts[0::2] + shell_counts[1::2]
    begins = starts[0::2]
    rows = jnp.arange(radial, dtype=jnp.int32)[None, None, :]

    def rows_of(places):
        row = jnp.where((places[None, :] >= 0) & (places[None, :] < totals[:, None]), begins[:, None] + places[None, :], -1)
        return (row[:, :, None] == rows).astype(kind).reshape(-1, radial)

    first = rows_of(slot)
    second = jnp.stack([
        rows_of(jnp.where(slot < slots // 2, slots + slot, -1)),
        rows_of(jnp.where(slot >= slots // 2, slots // 2 + slot, -1))])
    return pl.pallas_call(
        functools.partial(chip_kernel, n_az, n_rad),
        in_specs=[pl.BlockSpec(memory_space=pl.ANY)] + [pl.BlockSpec(memory_space=pltpu.VMEM)] * 5,
        out_specs=pl.BlockSpec(memory_space=pl.ANY),
        out_shape=jax.ShapeDtypeStruct((fields, n_az, slab, planes, block), kind),
        scratch_shapes=[
            pltpu.VMEM((fields, planes, slots, length), kind),
            pltpu.VMEM((n_rad, fields, slab, planes, slots), kind),
            pltpu.VMEM((chunks, n_rad, PART, planes // 2, slots), kind),
            pltpu.VMEM((n_rad, chunks, units, planes // 2, slots), kind),
            pltpu.VMEM((n_rad // 2, chunks, units, planes, slots), kind),
            pltpu.VMEM((fields, n_az, slab, planes, block), kind),
            pltpu.VMEM((fields, n_az, slab, planes, block), kind),
            pltpu.VMEM((fields, n_az, slab, planes, block), kind),
            dma((chunks,)), dma((chunks,)),
            dma((chunks, n_rad)), dma((chunks, n_rad)),
            dma((chunks, n_az)), dma((chunks, n_az)),
            dma((chunks, n_az)), dma((chunks, n_az)),
            dma((chunks, 3)), dma((fields,)),
        ],
        compiler_params=pltpu.CompilerParams(
            collective_id=1, has_side_effects=True, vmem_limit_bytes=VMEM_LIMIT),
    )(field, near, rest, first, second, cas_table)


def radial_kernel(modes_ref, ops_ref, which_ref, out_ref):
    _, blocks, slab, comps, block = modes_ref.shape
    radial = blocks * block
    rows = [modes_ref[0, b].reshape(slab * comps, block) for b in range(blocks)]
    rows = jnp.concatenate(rows, axis=1)
    mapped = []
    for n in range(2):
        whole = lax.dot_general(rows, ops_ref[n], (((1,), (1,)), ((), ())), preferred_element_type=jnp.float32)
        mapped.append(whole.reshape(slab, comps, radial))
    picked = jnp.where(which_ref[...] > 0, mapped[1], mapped[0])
    out_ref[:, 0] = jnp.swapaxes(picked, 0, 1).astype(out_ref.dtype)


def apply_radial(modes, radial_ops, chosen_ids):
    fields, blocks, slab, comps, block = modes.shape
    radial = blocks * block
    part = 16
    which = jnp.broadcast_to(chosen_ids[None, :, None], (1, comps, radial))
    return pl.pallas_call(
        radial_kernel,
        grid=(fields, comps // part),
        in_specs=[
            pl.BlockSpec((1, blocks, slab, part, block), lambda f, c: (f, 0, 0, c, 0)),
            pl.BlockSpec((2, radial, radial), lambda f, c: (0, 0, 0)),
            pl.BlockSpec((1, part, radial), lambda f, c: (0, c, 0)),
        ],
        out_specs=pl.BlockSpec((part, 1, slab, radial), lambda f, c: (c, f, 0, 0)),
        out_shape=jax.ShapeDtypeStruct((comps, fields, slab, radial), modes.dtype),
        compiler_params=pltpu.CompilerParams(vmem_limit_bytes=VMEM_LIMIT),
    )(modes, radial_ops, which)


def per_device(field, shell_counts, op_index, radial_ops):
    planes, fields, slots, cells = field.shape
    n_az, n_rad = lax.axis_size("az"), lax.axis_size("rad")
    comps_all = planes * n_az
    radial = radial_ops.shape[1]
    cas_table = make_table(comps_all)
    comp_ids = lax.axis_index("az") * planes + jnp.arange(planes, dtype=jnp.int32)
    mode_ids = jnp.minimum(comp_ids, comps_all - comp_ids)
    slab = cells // n_rad
    if slots % 128 or cells % 128 or n_rad % 4 or slab % 16 or planes % 32 or radial % (128 * n_az):
        row_slot = slot_index(shell_counts, slots, radial)
        return plain_path(field, row_slot, cas_table, jnp.take(op_index, mode_ids), radial_ops)
    shells = jnp.arange(n_rad, dtype=jnp.int32)
    starts = jnp.sum(jnp.where(shells[None, :] < shells[:, None], shell_counts[None, :], 0), axis=1)

    def any_counts():
        slot = jnp.arange(slots, dtype=jnp.int32)[None, :]
        row_of = jnp.where(slot < shell_counts[:, None], starts[:, None] + slot, -1)
        pack = row_of[:, :, None] == jnp.arange(radial, dtype=jnp.int32)[None, None, :]
        pack = pack.astype(field.dtype).reshape(n_rad * slots, radial)
        return exchange(field, pack, cas_table, n_az, n_rad)

    def even_counts():
        return exchange_packed(field, shell_counts, starts, radial, cas_table, n_az, n_rad)

    numbers = jnp.arange(op_index.shape[0], dtype=jnp.int32)
    chosen_ids = jnp.sum(jnp.where(mode_ids[:, None] == numbers[None, :], op_index[None, :], 0), axis=1)
    fullest = jnp.max(shell_counts[0::2] + shell_counts[1::2])
    modes = lax.cond(2 * fullest <= 3 * slots, even_counts, any_counts)
    return apply_radial(modes, radial_ops, chosen_ids)


def solution(mesh):
    return jax.shard_map(
        per_device,
        mesh=mesh,
        in_specs=(P("az", None, "rad", None), P(), P(), P()),
        out_specs=P("az", None, "rad", None),
        check_vma=False,
    )
```

```python
import functools
import math

import jax
import jax.numpy as jnp
from jax import lax
from jax.experimental import pallas as pl
from jax.experimental.pallas import tpu as pltpu
from jax.sharding import PartitionSpec as P

MESH = pl.DeviceIdType.MESH
VMEM_LIMIT = 60 << 20
PART = 4
AHEAD = 2


def make_table(length):
    index = jnp.arange(length, dtype=jnp.int32)
    product = index[:, None] * index[None, :] % length
    angle = product.astype(jnp.float32) * (2.0 * math.pi / length)
    return ((jnp.cos(angle) + jnp.sin(angle)) * (1.0 / math.sqrt(length))).astype(jnp.bfloat16)


def slot_index(counts, capacity, radial):
    starts = jnp.cumsum(counts) - counts
    rows = jnp.arange(radial, dtype=jnp.int32)
    owner = jnp.sum((starts[None, :] <= rows[:, None]).astype(jnp.int32), axis=1) - 1
    return owner * capacity + rows - jnp.take(starts, owner)


def to_planes(values):
    return lax.all_to_all(values, "az", split_axis=3, concat_axis=0, tiled=True)


def to_modes(values):
    return lax.all_to_all(values, "az", split_axis=0, concat_axis=3, tiled=True)


def regroup_shells(values):
    return lax.all_to_all(values, "rad", split_axis=3, concat_axis=2, tiled=True)


def transform(cas_table, values):
    shape = values.shape
    flat = jnp.dot(cas_table, values.reshape(shape[0], -1), preferred_element_type=jnp.float32)
    return flat.astype(jnp.bfloat16).reshape(shape)


def plain_path(field, row_slot, cas_table, chosen_ids, radial_ops):
    chosen = jnp.take(radial_ops, chosen_ids, axis=0)
    gathered = to_planes(field)
    spectra = transform(cas_table, gathered)
    returned = to_modes(spectra)
    slab_data = regroup_shells(returned)
    packed = jnp.take(slab_data, row_slot, axis=2)
    result = jnp.einsum("crs,cfsx->cfxr", chosen, packed, preferred_element_type=jnp.float32)
    return result.astype(jnp.bfloat16)


def one_hot(flags):
    return jnp.where(flags, 1.0, 0.0).astype(jnp.bfloat16)


def grids(rows, columns):
    return (lax.broadcasted_iota(jnp.int32, (rows, columns), 0),
            lax.broadcasted_iota(jnp.int32, (rows, columns), 1))


def whole_kernel(n_az, n_rad, paired, field_ref, counts_ref, cas_ref, ops_ref, second_op_ref, out_ref,
                 raw, cells, shells, packed, planes_in, spectra, modes, results, turned_ops, pack,
                 rad_send, rad_recv, az_send, az_recv, back_send, back_recv, own_sem, raw_sem, out_sem,
                 beside=None, outgoing=None, near=None, rest=None, second=None,
                 pair_send=None, pair_recv=None):
    az, rad = lax.axis_index("az"), lax.axis_index("rad")
    chip, core = rad // 2, rad % 2
    _, fields, slab, planes, slots = cells.shape
    block = packed.shape[4]
    radial = n_az * block
    half = planes // 2
    parts = slab // PART
    chunks = fields * parts
    chips = range(n_rad // 2)

    def raw_copy(f):
        return pltpu.make_async_copy(field_ref.at[:, f], raw.at[f % 2], raw_sem.at[f])

    def out_copy(f):
        return pltpu.make_async_copy(results.at[f % 2], out_ref.at[:, f], out_sem.at[f])

    raw_copy(0).start()
    raw_copy(1).start()

    barrier = pltpu.get_barrier_semaphore()
    for step in range(1, n_rad):
        pl.semaphore_signal(barrier, inc=1, device_id=(az, lax.rem(rad + step, n_rad)), device_id_type=MESH)
    for step in range(1, n_az):
        pl.semaphore_signal(barrier, inc=1, device_id=(lax.rem(az + step, n_az), rad), device_id_type=MESH)

    def place(q):
        return q // parts, pl.ds((q % parts) * PART, PART)

    def halves(which):
        return pl.ds(pl.multiple_of(which * half, half), half)

    def pair_copy(q):
        f, here = place(q)
        return pltpu.make_async_remote_copy(
            src_ref=cells.at[:, f, here, halves(1 - core)], dst_ref=beside.at[q],
            send_sem=pair_send.at[q], recv_sem=pair_recv.at[q],
            device_id=(az, chip * 2 + 1 - core), device_id_type=MESH)

    def rad_ends(q, to):
        if paired:
            return outgoing.at[to, q], shells.at[chip, q, :, halves(core)]
        f, here = place(q)
        return cells.at[to, f, here], shells.at[rad, f, here]

    def rad_copy(q, step):
        other = lax.rem(rad + step, n_rad)
        source, target = rad_ends(q, other)
        return pltpu.make_async_remote_copy(
            src_ref=source, dst_ref=target,
            send_sem=rad_send.at[q, step], recv_sem=rad_recv.at[q, step],
            device_id=(az, other), device_id_type=MESH)

    def az_copy(q, step):
        f, here = place(q)
        other = lax.rem(az + step, n_az)
        return pltpu.make_async_remote_copy(
            src_ref=packed.at[f, other, here], dst_ref=planes_in.at[f, az, here],
            send_sem=az_send.at[q, step], recv_sem=az_recv.at[q, step],
            device_id=(other, rad), device_id_type=MESH)

    def back_copy(q, step):
        f, here = place(q)
        other = lax.rem(az + step, n_az)
        return pltpu.make_async_remote_copy(
            src_ref=spectra.at[f, other, here], dst_ref=modes.at[f, az, here],
            send_sem=back_send.at[q, step], recv_sem=back_recv.at[q, step],
            device_id=(other, rad), device_id_type=MESH)

    def own_shells(q):
        return pltpu.make_async_copy(*rad_ends(q, rad), own_sem.at[q, 0])

    def own_planes(q):
        f, here = place(q)
        return pltpu.make_async_copy(packed.at[f, az, here], planes_in.at[f, az, here], own_sem.at[q, 1])

    def own_spectra(q):
        f, here = place(q)
        return pltpu.make_async_copy(spectra.at[f, az, here], modes.at[f, az, here], own_sem.at[q, 2])

    rad_steps = range(1, n_rad)
    az_steps = range(1, n_az)

    def lay_out(f):
        raw_copy(f).wait()

        @pl.loop(0, planes // 16)
        def _(part):
            here = pl.ds(pl.multiple_of(part * 16, 16), 16)
            turned = jnp.swapaxes(raw[f % 2, here], 1, 2)
            by_cell = jnp.swapaxes(turned, 0, 1)
            cells[:, f, :, here, :] = by_cell.reshape(n_rad, slab, 16, slots)

    def start_rad(q):
        f, here = place(q)
        if paired:
            pair_copy(q).wait_recv()

            @pl.loop(0, n_rad // 4)
            def _(group):
                to = pl.ds(group * 4, 4)
                mine = cells[to, f, here, halves(core)].reshape(4 * PART * half, slots)
                both = jnp.concatenate([mine, beside[q, to].reshape(4 * PART * half, slots)], axis=1)
                close = jnp.dot(both, near[...], preferred_element_type=jnp.float32)
                outgoing[to, q, :PART] = close.astype(jnp.bfloat16).reshape(4, PART, half, slots)
                split = both.reshape(4, PART, half, 2 * slots)
                ends = [split[:, :PART // 2], split[:, PART // 2:]]
                ends = [end.reshape(4 * PART // 2 * half, 2 * slots) for end in ends]
                more = jnp.dot(jnp.concatenate(ends, axis=1), rest[...], preferred_element_type=jnp.float32)
                outgoing[to, q, PART:] = more.astype(jnp.bfloat16).reshape(4, PART // 2, half, slots)

        for step in rad_steps:
            rad_copy(q, step).start()
        own_shells(q).start()

    def dense_rows(q):
        f, here = place(q)
        if not paired:
            rows = [shells[j, f, here].reshape(PART * planes, slots) for j in range(n_rad)]
            return jnp.dot(jnp.concatenate(rows, axis=1), pack[...], preferred_element_type=jnp.float32)
        rows = [shells[j, q, :PART].reshape(PART * planes, slots) for j in chips]
        dense = jnp.dot(jnp.concatenate(rows, axis=1), pack[...], preferred_element_type=jnp.float32)
        rows = [shells[j, q, PART:].reshape(PART // 2 * planes, slots) for j in chips]
        rows = jnp.concatenate(rows, axis=1)
        more = [jnp.dot(rows, second[n], preferred_element_type=jnp.float32) for n in range(2)]
        return dense + jnp.concatenate(more, axis=0)

    def finish(q):
        f, _ = place(q)
        for step in az_steps:
            az_copy(q, step).wait_recv()
        own_planes(q).wait()

        @pl.loop(0, PART // 2)
        def _(pair):
            first = (q % parts) * PART + pair * 2
            both = [planes_in[f, :, first + x].reshape(n_az * planes, block) for x in range(2)]
            found = jnp.dot(cas_ref[...], jnp.concatenate(both, axis=1), preferred_element_type=jnp.float32)
            found = found.astype(jnp.bfloat16)
            for x in range(2):
                for k in range(n_az):
                    spectra[f, k, first + x] = found[k * planes:(k + 1) * planes, x * block:(x + 1) * block]

        for step in az_steps:
            back_copy(q, step).start()
        own_spectra(q).start()

    def apply_radial(f):
        @pl.loop(0, parts)
        def _(part):
            for step in az_steps:
                back_copy(f * parts + part, step).wait_recv()
            own_spectra(f * parts + part).wait()

        @pl.when(f >= 2)
        def _():
            out_copy(f - 2).wait()

        @pl.loop(0, planes // 16)
        def _(part):
            here = pl.ds(pl.multiple_of(part * 16, 16), 16)
            takes_second = second_op_ref[here]
            both = [[], []]
            for b in range(n_az):
                by_mode = jnp.swapaxes(modes[f, b, :, here], 0, 1)
                later = by_mode * takes_second
                both[0].append((by_mode - later).reshape(16 * slab, block))
                both[1].append(later.reshape(16 * slab, block))
            rows = jnp.concatenate(both[0] + both[1], axis=1)
            mapped = jnp.dot(rows, turned_ops[...], preferred_element_type=jnp.float32)
            results[f % 2, here] = mapped.astype(jnp.bfloat16).reshape(16, slab, radial)

        out_copy(f).start()

    counts = [counts_ref[j] for j in range(n_rad)]
    starts = [0 * counts[0]]
    for j in range(1, n_rad):
        starts.append(starts[-1] + counts[j - 1])

    if paired:
        row, column = grids(slots, slots)
        low = slots // 2
        mine, theirs = counts_ref[rad], counts_ref[chip * 2 + 1 - core]
        for n, (count, offset) in enumerate([(mine, core * theirs), (theirs, (1 - core) * mine)]):
            spot, held = row + offset, row < count
            near[n * slots:(n + 1) * slots, :] = one_hot((spot == column) & held)
            rest[n * slots:(n + 1) * slots, :] = one_hot((spot == slots + column) & held & (column < low))
            rest[(n + 2) * slots:(n + 3) * slots, :] = one_hot((spot == low + column) & held & (column >= low))

    lay_out(0)
    pl.semaphore_wait(barrier, n_rad + n_az - 2)
    if paired:
        for q in range(parts):
            pair_copy(q).start()

    @pl.loop(0, AHEAD)
    def _(q):
        start_rad(q)

    row, column = grids(slots, radial)
    if paired:
        for j in chips:
            begin, total, here = starts[2 * j], counts[2 * j] + counts[2 * j + 1], slice(j * slots, (j + 1) * slots)
            pack[here, :] = one_hot((row + begin == column) & (row < total))
            after = row + slots
            second[0, here, :] = one_hot((after + begin == column) & (after < total) & (row < low))
            after = row + low
            second[1, here, :] = one_hot((after + begin == column) & (after < total) & (row >= low))
    else:
        for j in range(n_rad):
            pack[j * slots:(j + 1) * slots, :] = one_hot((row + starts[j] == column) & (row < counts[j]))
    for n in range(2):
        turned_ops[n * radial:(n + 1) * radial, :] = ops_ref[n].T

    @pl.loop(0, chunks)
    def _(q):
        f, here = place(q)

        @pl.when((q % parts == 0) & (f + 1 < fields))
        def _():
            @pl.when(f + 2 < fields)
            def _():
                raw_copy(f + 2).start()

            lay_out(f + 1)
            if paired:
                for part in range(parts):
                    pair_copy(q + parts + part).start()

        @pl.when(q + AHEAD < chunks)
        def _():
            start_rad(q + AHEAD)

        for step in rad_steps:
            rad_copy(q, step).wait_recv()
        own_shells(q).wait()
        dense = dense_rows(q).astype(jnp.bfloat16)
        for k in range(n_az):
            packed[f, k, here] = dense[:, k * block:(k + 1) * block].reshape(PART, planes, block)

        for step in az_steps:
            az_copy(q, step).start()
        own_planes(q).start()

        @pl.when(q > 0)
        def _():
            finish(q - 1)

        @pl.when((q % parts == parts // 2) & (f > 0))
        def _():
            apply_radial(f - 1)

    finish(chunks - 1)
    apply_radial(fields - 1)

    @pl.loop(0, chunks)
    def _(q):
        if paired:
            pair_copy(q).wait_send()
        for step in rad_steps:
            rad_copy(q, step).wait_send()
        for step in az_steps:
            az_copy(q, step).wait_send()
            back_copy(q, step).wait_send()

    out_copy(fields - 2).wait()
    out_copy(fields - 1).wait()


def whole(field, shell_counts, cas_table, radial_ops, second_op, n_az, n_rad, paired):
    planes, fields, slots, length = field.shape
    slab = length // n_rad
    radial = radial_ops.shape[1]
    block = radial // n_az
    chunks = fields * slab // PART
    units = PART + PART // 2
    kind = field.dtype
    dma = pltpu.SemaphoreType.DMA
    spread = pltpu.VMEM((fields, n_az, slab, planes, block), kind)
    if paired:
        shells = pltpu.VMEM((n_rad // 2, chunks, units, planes, slots), kind)
        extra = [
            pltpu.VMEM((chunks, n_rad, PART, planes // 2, slots), kind),
            pltpu.VMEM((n_rad, chunks, units, planes // 2, slots), kind),
            pltpu.VMEM((2 * slots, slots), kind),
            pltpu.VMEM((4 * slots, slots), kind),
            pltpu.VMEM((2, n_rad // 2 * slots, radial), kind),
            dma((chunks,)), dma((chunks,)),
        ]
    else:
        shells = pltpu.VMEM((n_rad, fields, slab, planes, slots), kind)
        extra = []
    vmem = pl.BlockSpec(memory_space=pltpu.VMEM)
    return pl.pallas_call(
        functools.partial(whole_kernel, n_az, n_rad, paired),
        in_specs=[pl.BlockSpec(memory_space=pl.ANY), pl.BlockSpec(memory_space=pltpu.SMEM), vmem, vmem, vmem],
        out_specs=pl.BlockSpec(memory_space=pl.ANY),
        out_shape=jax.ShapeDtypeStruct((planes, fields, slab, radial), kind),
        scratch_shapes=[
            pltpu.VMEM((2, planes, slots, length), kind),
            pltpu.VMEM((n_rad, fields, slab, planes, slots), kind),
            shells, spread, spread, spread, spread,
            pltpu.VMEM((2, planes, slab, radial), kind),
            pltpu.VMEM((2 * radial, radial), kind),
            pltpu.VMEM((n_rad * slots // (2 if paired else 1), radial), kind),
            dma((chunks, n_rad)), dma((chunks, n_rad)),
            dma((chunks, n_az)), dma((chunks, n_az)),
            dma((chunks, n_az)), dma((chunks, n_az)),
            dma((chunks, 3)), dma((fields,)), dma((fields,)),
        ] + extra,
        compiler_params=pltpu.CompilerParams(
            collective_id=1 if paired else 0, has_side_effects=True, vmem_limit_bytes=VMEM_LIMIT),
    )(field, shell_counts, cas_table, radial_ops, second_op)


def per_device(field, shell_counts, op_index, radial_ops):
    planes, fields, slots, cells = field.shape
    n_az, n_rad = lax.axis_size("az"), lax.axis_size("rad")
    comps_all = planes * n_az
    radial = radial_ops.shape[1]
    cas_table = make_table(comps_all)
    comp_ids = lax.axis_index("az") * planes + jnp.arange(planes, dtype=jnp.int32)
    mode_ids = jnp.minimum(comp_ids, comps_all - comp_ids)
    slab = cells // n_rad
    if fields < 2 or slots % 128 or cells % 128 or n_rad % 4 or slab % 16 or planes % 32 or radial % (128 * n_az):
        row_slot = slot_index(shell_counts, slots, radial)
        return plain_path(field, row_slot, cas_table, jnp.take(op_index, mode_ids), radial_ops)
    numbers = jnp.arange(op_index.shape[0], dtype=jnp.int32)
    chosen_ids = jnp.sum(jnp.where(mode_ids[:, None] == numbers[None, :], op_index[None, :], 0), axis=1)
    second_op = jnp.broadcast_to(chosen_ids[:, None, None], (planes, slab, radial // n_az)).astype(field.dtype)
    chips = jnp.arange(n_rad, dtype=jnp.int32) // 2
    together = jnp.sum(jnp.where(chips[:, None] == chips[None, :], shell_counts[None, :], 0), axis=1)
    operands = (field, shell_counts, cas_table, radial_ops, second_op)
    return lax.cond(
        2 * jnp.max(together) <= 3 * slots,
        lambda *given: whole(*given, n_az, n_rad, True),
        lambda *given: whole(*given, n_az, n_rad, False),
        *operands)


def solution(mesh):
    return jax.shard_map(
        per_device,
        mesh=mesh,
        in_specs=(P("az", None, "rad", None), P(), P(), P()),
        out_specs=P("az", None, "rad", None),
        check_vma=False,
    )
```

```python
import functools
import math

import jax
import jax.numpy as jnp
from jax import lax
from jax.experimental import pallas as pl
from jax.experimental.pallas import tpu as pltpu
from jax.sharding import PartitionSpec as P

MESH = pl.DeviceIdType.MESH
VMEM_LIMIT = 60 << 20
PART = 4
AHEAD = 1


def make_table(length):
    index = jnp.arange(length, dtype=jnp.int32)
    product = index[:, None] * index[None, :] % length
    angle = product.astype(jnp.float32) * (2.0 * math.pi / length)
    return ((jnp.cos(angle) + jnp.sin(angle)) * (1.0 / math.sqrt(length))).astype(jnp.bfloat16)


def slot_index(counts, capacity, radial):
    starts = jnp.cumsum(counts) - counts
    rows = jnp.arange(radial, dtype=jnp.int32)
    owner = jnp.sum((starts[None, :] <= rows[:, None]).astype(jnp.int32), axis=1) - 1
    return owner * capacity + rows - jnp.take(starts, owner)


def to_planes(values):
    return lax.all_to_all(values, "az", split_axis=3, concat_axis=0, tiled=True)


def to_modes(values):
    return lax.all_to_all(values, "az", split_axis=0, concat_axis=3, tiled=True)


def regroup_shells(values):
    return lax.all_to_all(values, "rad", split_axis=3, concat_axis=2, tiled=True)


def transform(cas_table, values):
    shape = values.shape
    flat = jnp.dot(cas_table, values.reshape(shape[0], -1), preferred_element_type=jnp.float32)
    return flat.astype(jnp.bfloat16).reshape(shape)


def plain_path(field, row_slot, cas_table, chosen_ids, radial_ops):
    chosen = jnp.take(radial_ops, chosen_ids, axis=0)
    gathered = to_planes(field)
    spectra = transform(cas_table, gathered)
    returned = to_modes(spectra)
    slab_data = regroup_shells(returned)
    packed = jnp.take(slab_data, row_slot, axis=2)
    result = jnp.einsum("crs,cfsx->cfxr", chosen, packed, preferred_element_type=jnp.float32)
    return result.astype(jnp.bfloat16)


def one_hot(flags):
    return jnp.where(flags, 1.0, 0.0).astype(jnp.bfloat16)


def grids(rows, columns):
    return (lax.broadcasted_iota(jnp.int32, (rows, columns), 0),
            lax.broadcasted_iota(jnp.int32, (rows, columns), 1))


def whole_kernel(n_az, n_rad, paired, field_ref, counts_ref, cas_ref, ops_ref, second_op_ref, out_ref,
                 raw, cells, shells, packed, planes_in, spectra, modes, results, turned_ops, pack,
                 rad_send, rad_recv, az_send, az_recv, back_send, back_recv, own_sem, raw_sem, out_sem,
                 beside=None, outgoing=None, near=None, rest=None, second=None,
                 pair_send=None, pair_recv=None):
    az, rad = lax.axis_index("az"), lax.axis_index("rad")
    chip, core = rad // 2, rad % 2
    _, fields, slab, planes, slots = cells.shape
    block = packed.shape[4]
    radial = n_az * block
    half = planes // 2
    parts = slab // PART
    chunks = fields * parts
    chips = range(n_rad // 2)

    def raw_copy(f):
        return pltpu.make_async_copy(field_ref.at[:, f], raw.at[f % 2], raw_sem.at[f])

    def out_copy(f):
        return pltpu.make_async_copy(results.at[f % 2], out_ref.at[:, f], out_sem.at[f])

    raw_copy(0).start()
    raw_copy(1).start()

    barrier = pltpu.get_barrier_semaphore()
    for step in range(1, n_rad):
        pl.semaphore_signal(barrier, inc=1, device_id=(az, lax.rem(rad + step, n_rad)), device_id_type=MESH)
    for step in range(1, n_az):
        pl.semaphore_signal(barrier, inc=1, device_id=(lax.rem(az + step, n_az), rad), device_id_type=MESH)

    def place(q):
        return q // parts, pl.ds((q % parts) * PART, PART)

    def halves(which):
        return pl.ds(pl.multiple_of(which * half, half), half)

    def pair_copy(q):
        f, here = place(q)
        return pltpu.make_async_remote_copy(
            src_ref=cells.at[:, f, here, halves(1 - core)], dst_ref=beside.at[q],
            send_sem=pair_send.at[q], recv_sem=pair_recv.at[q],
            device_id=(az, chip * 2 + 1 - core), device_id_type=MESH)

    def rad_ends(q, to):
        if paired:
            return outgoing.at[to, q], shells.at[chip, q, :, halves(core)]
        f, here = place(q)
        return cells.at[to, f, here], shells.at[rad, f, here]

    def rad_copy(q, step):
        other = lax.rem(rad + step, n_rad)
        source, target = rad_ends(q, other)
        return pltpu.make_async_remote_copy(
            src_ref=source, dst_ref=target,
            send_sem=rad_send.at[q, step], recv_sem=rad_recv.at[q, step],
            device_id=(az, other), device_id_type=MESH)

    def az_copy(q, step):
        f, here = place(q)
        other = lax.rem(az + step, n_az)
        return pltpu.make_async_remote_copy(
            src_ref=packed.at[f, other, here], dst_ref=planes_in.at[f, az, here],
            send_sem=az_send.at[q, step], recv_sem=az_recv.at[q, step],
            device_id=(other, rad), device_id_type=MESH)

    def back_copy(q, step):
        f, here = place(q)
        other = lax.rem(az + step, n_az)
        return pltpu.make_async_remote_copy(
            src_ref=spectra.at[f, other, here], dst_ref=modes.at[f, az, here],
            send_sem=back_send.at[q, step], recv_sem=back_recv.at[q, step],
            device_id=(other, rad), device_id_type=MESH)

    def own_shells(q):
        return pltpu.make_async_copy(*rad_ends(q, rad), own_sem.at[q, 0])

    def own_planes(q):
        f, here = place(q)
        return pltpu.make_async_copy(packed.at[f, az, here], planes_in.at[f, az, here], own_sem.at[q, 1])

    def own_spectra(q):
        f, here = place(q)
        return pltpu.make_async_copy(spectra.at[f, az, here], modes.at[f, az, here], own_sem.at[q, 2])

    rad_steps = range(1, n_rad)
    az_steps = range(1, n_az)

    def lay_out(f):
        raw_copy(f).wait()

        @pl.loop(0, planes // 16)
        def _(part):
            here = pl.ds(pl.multiple_of(part * 16, 16), 16)
            turned = jnp.swapaxes(raw[f % 2, here], 1, 2)
            by_cell = jnp.swapaxes(turned, 0, 1)
            cells[:, f, :, here, :] = by_cell.reshape(n_rad, slab, 16, slots)

    def start_rad(q):
        f, here = place(q)
        if paired:
            pair_copy(q).wait_recv()

            @pl.loop(0, n_rad // 4)
            def _(group):
                to = pl.ds(group * 4, 4)
                mine = cells[to, f, here, halves(core)].reshape(4 * PART * half, slots)
                both = jnp.concatenate([mine, beside[q, to].reshape(4 * PART * half, slots)], axis=1)
                close = jnp.dot(both, near[...], preferred_element_type=jnp.float32)
                outgoing[to, q, :PART] = close.astype(jnp.bfloat16).reshape(4, PART, half, slots)
                split = both.reshape(4, PART, half, 2 * slots)
                ends = [split[:, :PART // 2], split[:, PART // 2:]]
                ends = [end.reshape(4 * PART // 2 * half, 2 * slots) for end in ends]
                more = jnp.dot(jnp.concatenate(ends, axis=1), rest[...], preferred_element_type=jnp.float32)
                outgoing[to, q, PART:] = more.astype(jnp.bfloat16).reshape(4, PART // 2, half, slots)

        for step in rad_steps:
            rad_copy(q, step).start()
        own_shells(q).start()

    def dense_rows(q):
        f, here = place(q)
        if not paired:
            rows = [shells[j, f, here].reshape(PART * planes, slots) for j in range(n_rad)]
            return jnp.dot(jnp.concatenate(rows, axis=1), pack[...], preferred_element_type=jnp.float32)
        rows = [shells[j, q, :PART].reshape(PART * planes, slots) for j in chips]
        dense = jnp.dot(jnp.concatenate(rows, axis=1), pack[...], preferred_element_type=jnp.float32)
        rows = [shells[j, q, PART:].reshape(PART // 2 * planes, slots) for j in chips]
        rows = jnp.concatenate(rows, axis=1)
        more = [jnp.dot(rows, second[n], preferred_element_type=jnp.float32) for n in range(2)]
        return dense + jnp.concatenate(more, axis=0)

    def finish(q):
        f, _ = place(q)
        for step in az_steps:
            az_copy(q, step).wait_recv()
        own_planes(q).wait()

        @pl.loop(0, PART // 2)
        def _(pair):
            first = (q % parts) * PART + pair * 2
            both = [planes_in[f, :, first + x].reshape(n_az * planes, block) for x in range(2)]
            found = jnp.dot(cas_ref[...], jnp.concatenate(both, axis=1), preferred_element_type=jnp.float32)
            found = found.astype(jnp.bfloat16)
            for x in range(2):
                for k in range(n_az):
                    spectra[f, k, first + x] = found[k * planes:(k + 1) * planes, x * block:(x + 1) * block]

        for step in az_steps:
            back_copy(q, step).start()
        own_spectra(q).start()

    def apply_radial(f):
        @pl.loop(0, parts)
        def _(part):
            for step in az_steps:
                back_copy(f * parts + part, step).wait_recv()
            own_spectra(f * parts + part).wait()

        @pl.when(f >= 2)
        def _():
            out_copy(f - 2).wait()

        @pl.loop(0, planes // 16)
        def _(part):
            here = pl.ds(pl.multiple_of(part * 16, 16), 16)
            takes_second = second_op_ref[here]
            both = [[], []]
            for b in range(n_az):
                by_mode = jnp.swapaxes(modes[f, b, :, here], 0, 1)
                later = by_mode * takes_second
                both[0].append((by_mode - later).reshape(16 * slab, block))
                both[1].append(later.reshape(16 * slab, block))
            rows = jnp.concatenate(both[0] + both[1], axis=1)
            mapped = jnp.dot(rows, turned_ops[...], preferred_element_type=jnp.float32)
            results[f % 2, here] = mapped.astype(jnp.bfloat16).reshape(16, slab, radial)

        out_copy(f).start()

    counts = [counts_ref[j] for j in range(n_rad)]
    starts = [0 * counts[0]]
    for j in range(1, n_rad):
        starts.append(starts[-1] + counts[j - 1])

    if paired:
        row, column = grids(slots, slots)
        low = slots // 2
        mine, theirs = counts_ref[rad], counts_ref[chip * 2 + 1 - core]
        for n, (count, offset) in enumerate([(mine, core * theirs), (theirs, (1 - core) * mine)]):
            spot, held = row + offset, row < count
            near[n * slots:(n + 1) * slots, :] = one_hot((spot == column) & held)
            rest[n * slots:(n + 1) * slots, :] = one_hot((spot == slots + column) & held & (column < low))
            rest[(n + 2) * slots:(n + 3) * slots, :] = one_hot((spot == low + column) & held & (column >= low))

    lay_out(0)
    pl.semaphore_wait(barrier, n_rad + n_az - 2)
    if paired:
        for q in range(parts):
            pair_copy(q).start()

    @pl.loop(0, AHEAD)
    def _(q):
        start_rad(q)

    row, column = grids(slots, radial)
    if paired:
        for j in chips:
            begin, total, here = starts[2 * j], counts[2 * j] + counts[2 * j + 1], slice(j * slots, (j + 1) * slots)
            pack[here, :] = one_hot((row + begin == column) & (row < total))
            after = row + slots
            second[0, here, :] = one_hot((after + begin == column) & (after < total) & (row < low))
            after = row + low
            second[1, here, :] = one_hot((after + begin == column) & (after < total) & (row >= low))
    else:
        for j in range(n_rad):
            pack[j * slots:(j + 1) * slots, :] = one_hot((row + starts[j] == column) & (row < counts[j]))
    for n in range(2):
        turned_ops[n * radial:(n + 1) * radial, :] = ops_ref[n].T

    @pl.loop(0, chunks)
    def _(q):
        f, here = place(q)

        @pl.when((q % parts == 0) & (f + 1 < fields))
        def _():
            @pl.when(f + 2 < fields)
            def _():
                raw_copy(f + 2).start()

            lay_out(f + 1)
            if paired:
                for part in range(parts):
                    pair_copy(q + parts + part).start()

        @pl.when(q + AHEAD < chunks)
        def _():
            start_rad(q + AHEAD)

        for step in rad_steps:
            rad_copy(q, step).wait_recv()
        own_shells(q).wait()
        dense = dense_rows(q).astype(jnp.bfloat16)
        for k in range(n_az):
            packed[f, k, here] = dense[:, k * block:(k + 1) * block].reshape(PART, planes, block)

        for step in az_steps:
            az_copy(q, step).start()
        own_planes(q).start()

        @pl.when(q > 0)
        def _():
            finish(q - 1)

        @pl.when((q % parts == parts // 2) & (f > 0))
        def _():
            apply_radial(f - 1)

    finish(chunks - 1)
    apply_radial(fields - 1)

    @pl.loop(0, chunks)
    def _(q):
        if paired:
            pair_copy(q).wait_send()
        for step in rad_steps:
            rad_copy(q, step).wait_send()
        for step in az_steps:
            az_copy(q, step).wait_send()
            back_copy(q, step).wait_send()

    out_copy(fields - 2).wait()
    out_copy(fields - 1).wait()


def whole(field, shell_counts, cas_table, radial_ops, second_op, n_az, n_rad, paired):
    planes, fields, slots, length = field.shape
    slab = length // n_rad
    radial = radial_ops.shape[1]
    block = radial // n_az
    chunks = fields * slab // PART
    units = PART + PART // 2
    kind = field.dtype
    dma = pltpu.SemaphoreType.DMA
    spread = pltpu.VMEM((fields, n_az, slab, planes, block), kind)
    if paired:
        shells = pltpu.VMEM((n_rad // 2, chunks, units, planes, slots), kind)
        extra = [
            pltpu.VMEM((chunks, n_rad, PART, planes // 2, slots), kind),
            pltpu.VMEM((n_rad, chunks, units, planes // 2, slots), kind),
            pltpu.VMEM((2 * slots, slots), kind),
            pltpu.VMEM((4 * slots, slots), kind),
            pltpu.VMEM((2, n_rad // 2 * slots, radial), kind),
            dma((chunks,)), dma((chunks,)),
        ]
    else:
        shells = pltpu.VMEM((n_rad, fields, slab, planes, slots), kind)
        extra = []
    vmem = pl.BlockSpec(memory_space=pltpu.VMEM)
    return pl.pallas_call(
        functools.partial(whole_kernel, n_az, n_rad, paired),
        in_specs=[pl.BlockSpec(memory_space=pl.ANY), pl.BlockSpec(memory_space=pltpu.SMEM), vmem, vmem, vmem],
        out_specs=pl.BlockSpec(memory_space=pl.ANY),
        out_shape=jax.ShapeDtypeStruct((planes, fields, slab, radial), kind),
        scratch_shapes=[
            pltpu.VMEM((2, planes, slots, length), kind),
            pltpu.VMEM((n_rad, fields, slab, planes, slots), kind),
            shells, spread, spread, spread, spread,
            pltpu.VMEM((2, planes, slab, radial), kind),
            pltpu.VMEM((2 * radial, radial), kind),
            pltpu.VMEM((n_rad * slots // (2 if paired else 1), radial), kind),
            dma((chunks, n_rad)), dma((chunks, n_rad)),
            dma((chunks, n_az)), dma((chunks, n_az)),
            dma((chunks, n_az)), dma((chunks, n_az)),
            dma((chunks, 3)), dma((fields,)), dma((fields,)),
        ] + extra,
        compiler_params=pltpu.CompilerParams(
            collective_id=1 if paired else 0, has_side_effects=True, vmem_limit_bytes=VMEM_LIMIT),
    )(field, shell_counts, cas_table, radial_ops, second_op)


def hand_over_kernel(from_ref, to_ref):
    to_ref[...] = from_ref[...]


def hand_over(result):
    block = (result.shape[0] // 4,) + result.shape[1:]
    spec = pl.BlockSpec(block, lambda n: (n, 0, 0, 0))
    return pl.pallas_call(
        hand_over_kernel,
        grid=(4,),
        in_specs=[spec],
        out_specs=spec,
        out_shape=jax.ShapeDtypeStruct(result.shape, result.dtype),
        compiler_params=pltpu.CompilerParams(vmem_limit_bytes=VMEM_LIMIT),
    )(result)


def per_device(field, shell_counts, op_index, radial_ops):
    planes, fields, slots, cells = field.shape
    n_az, n_rad = lax.axis_size("az"), lax.axis_size("rad")
    comps_all = planes * n_az
    radial = radial_ops.shape[1]
    cas_table = make_table(comps_all)
    comp_ids = lax.axis_index("az") * planes + jnp.arange(planes, dtype=jnp.int32)
    mode_ids = jnp.minimum(comp_ids, comps_all - comp_ids)
    slab = cells // n_rad
    if fields < 2 or slots % 128 or cells % 128 or n_rad % 4 or slab % 16 or planes % 32 or radial % (128 * n_az):
        row_slot = slot_index(shell_counts, slots, radial)
        return plain_path(field, row_slot, cas_table, jnp.take(op_index, mode_ids), radial_ops)
    numbers = jnp.arange(op_index.shape[0], dtype=jnp.int32)
    chosen_ids = jnp.sum(jnp.where(mode_ids[:, None] == numbers[None, :], op_index[None, :], 0), axis=1)
    second_op = jnp.broadcast_to(chosen_ids[:, None, None], (planes, slab, radial // n_az)).astype(field.dtype)
    chips = jnp.arange(n_rad, dtype=jnp.int32) // 2
    together = jnp.sum(jnp.where(chips[:, None] == chips[None, :], shell_counts[None, :], 0), axis=1)
    operands = (field, shell_counts, cas_table, radial_ops, second_op)
    result = lax.cond(
        2 * jnp.max(together) <= 3 * slots,
        lambda *given: whole(*given, n_az, n_rad, True),
        lambda *given: whole(*given, n_az, n_rad, False),
        *operands)
    return hand_over(result)


def solution(mesh):
    return jax.shard_map(
        per_device,
        mesh=mesh,
        in_specs=(P("az", None, "rad", None), P(), P(), P()),
        out_specs=P("az", None, "rad", None),
        check_vma=False,
    )
```

```python
import functools
import math

import jax
import jax.numpy as jnp
from jax import lax
from jax.experimental import pallas as pl
from jax.experimental.pallas import tpu as pltpu
from jax.sharding import PartitionSpec as P

MESH = pl.DeviceIdType.MESH
VMEM_LIMIT = 60 << 20
PART = 4
AHEAD = 1


def make_table(length):
    index = jnp.arange(length, dtype=jnp.int32)
    product = index[:, None] * index[None, :] % length
    angle = product.astype(jnp.float32) * (2.0 * math.pi / length)
    return ((jnp.cos(angle) + jnp.sin(angle)) * (1.0 / math.sqrt(length))).astype(jnp.bfloat16)


def slot_index(counts, capacity, radial):
    starts = jnp.cumsum(counts) - counts
    rows = jnp.arange(radial, dtype=jnp.int32)
    owner = jnp.sum((starts[None, :] <= rows[:, None]).astype(jnp.int32), axis=1) - 1
    return owner * capacity + rows - jnp.take(starts, owner)


def to_planes(values):
    return lax.all_to_all(values, "az", split_axis=3, concat_axis=0, tiled=True)


def to_modes(values):
    return lax.all_to_all(values, "az", split_axis=0, concat_axis=3, tiled=True)


def regroup_shells(values):
    return lax.all_to_all(values, "rad", split_axis=3, concat_axis=2, tiled=True)


def transform(cas_table, values):
    shape = values.shape
    flat = jnp.dot(cas_table, values.reshape(shape[0], -1), preferred_element_type=jnp.float32)
    return flat.astype(jnp.bfloat16).reshape(shape)


def plain_path(field, row_slot, cas_table, chosen_ids, radial_ops):
    chosen = jnp.take(radial_ops, chosen_ids, axis=0)
    gathered = to_planes(field)
    spectra = transform(cas_table, gathered)
    returned = to_modes(spectra)
    slab_data = regroup_shells(returned)
    packed = jnp.take(slab_data, row_slot, axis=2)
    result = jnp.einsum("crs,cfsx->cfxr", chosen, packed, preferred_element_type=jnp.float32)
    return result.astype(jnp.bfloat16)


def one_hot(flags):
    return jnp.where(flags, 1.0, 0.0).astype(jnp.bfloat16)


def grids(rows, columns):
    return (lax.broadcasted_iota(jnp.int32, (rows, columns), 0),
            lax.broadcasted_iota(jnp.int32, (rows, columns), 1))


def whole_kernel(n_az, n_rad, paired, field_ref, counts_ref, cas_ref, ops_ref, second_op_ref, out_ref,
                 raw, cells, shells, packed, planes_in, spectra, modes, results, turned_ops, pack,
                 rad_send, rad_recv, az_send, az_recv, back_send, back_recv, own_sem, raw_sem, out_sem,
                 beside=None, outgoing=None, near=None, rest=None, second=None,
                 pair_send=None, pair_recv=None):
    az, rad = lax.axis_index("az"), lax.axis_index("rad")
    chip, core = rad // 2, rad % 2
    _, fields, slab, planes, slots = cells.shape
    block = packed.shape[4]
    radial = n_az * block
    half = planes // 2
    parts = slab // PART
    chunks = fields * parts
    chips = range(n_rad // 2)

    def raw_copy(f):
        return pltpu.make_async_copy(field_ref.at[:, f], raw.at[f % 2], raw_sem.at[f])

    def out_copy(f):
        return pltpu.make_async_copy(results.at[f % 2], out_ref.at[:, f], out_sem.at[f])

    raw_copy(0).start()
    raw_copy(1).start()

    barrier = pltpu.get_barrier_semaphore()
    for step in range(1, n_rad):
        pl.semaphore_signal(barrier, inc=1, device_id=(az, lax.rem(rad + step, n_rad)), device_id_type=MESH)
    for step in range(1, n_az):
        pl.semaphore_signal(barrier, inc=1, device_id=(lax.rem(az + step, n_az), rad), device_id_type=MESH)

    def place(q):
        return q // parts, pl.ds((q % parts) * PART, PART)

    def halves(which):
        return pl.ds(pl.multiple_of(which * half, half), half)

    def pair_copy(q):
        f, here = place(q)
        return pltpu.make_async_remote_copy(
            src_ref=cells.at[:, f, here, halves(1 - core)], dst_ref=beside.at[q],
            send_sem=pair_send.at[q], recv_sem=pair_recv.at[q],
            device_id=(az, chip * 2 + 1 - core), device_id_type=MESH)

    def rad_ends(q, to):
        if paired:
            return outgoing.at[to, q], shells.at[chip, q, :, halves(core)]
        f, here = place(q)
        return cells.at[to, f, here], shells.at[rad, f, here]

    def rad_copy(q, step):
        other = lax.rem(rad + step, n_rad)
        source, target = rad_ends(q, other)
        return pltpu.make_async_remote_copy(
            src_ref=source, dst_ref=target,
            send_sem=rad_send.at[q, step], recv_sem=rad_recv.at[q, step],
            device_id=(az, other), device_id_type=MESH)

    def az_copy(q, step):
        f, here = place(q)
        other = lax.rem(az + step, n_az)
        return pltpu.make_async_remote_copy(
            src_ref=packed.at[f, other, here], dst_ref=planes_in.at[f, az, here],
            send_sem=az_send.at[q, step], recv_sem=az_recv.at[q, step],
            device_id=(other, rad), device_id_type=MESH)

    def back_copy(q, step):
        f, here = place(q)
        other = lax.rem(az + step, n_az)
        return pltpu.make_async_remote_copy(
            src_ref=spectra.at[f, other, here], dst_ref=modes.at[f, az, here],
            send_sem=back_send.at[q, step], recv_sem=back_recv.at[q, step],
            device_id=(other, rad), device_id_type=MESH)

    def own_shells(q):
        return pltpu.make_async_copy(*rad_ends(q, rad), own_sem.at[q, 0])

    def own_planes(q):
        f, here = place(q)
        return pltpu.make_async_copy(packed.at[f, az, here], planes_in.at[f, az, here], own_sem.at[q, 1])

    def own_spectra(q):
        f, here = place(q)
        return pltpu.make_async_copy(spectra.at[f, az, here], modes.at[f, az, here], own_sem.at[q, 2])

    rad_steps = range(1, n_rad)
    az_steps = range(1, n_az)

    def lay_out(f):
        raw_copy(f).wait()

        @pl.loop(0, planes // 16)
        def _(part):
            here = pl.ds(pl.multiple_of(part * 16, 16), 16)
            turned = jnp.swapaxes(raw[f % 2, here], 1, 2)
            by_cell = jnp.swapaxes(turned, 0, 1)
            cells[:, f, :, here, :] = by_cell.reshape(n_rad, slab, 16, slots)

    def start_rad(q):
        f, here = place(q)
        if paired:
            pair_copy(q).wait_recv()

            @pl.loop(0, n_rad // 4)
            def _(group):
                to = pl.ds(group * 4, 4)
                mine = cells[to, f, here, halves(core)].reshape(4 * PART * half, slots)
                both = jnp.concatenate([mine, beside[q, to].reshape(4 * PART * half, slots)], axis=1)
                close = jnp.dot(both, near[...], preferred_element_type=jnp.float32)
                outgoing[to, q, :PART] = close.astype(jnp.bfloat16).reshape(4, PART, half, slots)
                split = both.reshape(4, PART, half, 2 * slots)
                ends = [split[:, :PART // 2], split[:, PART // 2:]]
                ends = [end.reshape(4 * PART // 2 * half, 2 * slots) for end in ends]
                more = jnp.dot(jnp.concatenate(ends, axis=1), rest[...], preferred_element_type=jnp.float32)
                outgoing[to, q, PART:] = more.astype(jnp.bfloat16).reshape(4, PART // 2, half, slots)

        for step in rad_steps:
            rad_copy(q, step).start()
        own_shells(q).start()

    def dense_rows(q):
        f, here = place(q)
        if not paired:
            rows = [shells[j, f, here].reshape(PART * planes, slots) for j in range(n_rad)]
            return jnp.dot(jnp.concatenate(rows, axis=1), pack[...], preferred_element_type=jnp.float32)
        rows = [shells[j, q, :PART].reshape(PART * planes, slots) for j in chips]
        dense = jnp.dot(jnp.concatenate(rows, axis=1), pack[...], preferred_element_type=jnp.float32)
        rows = [shells[j, q, PART:].reshape(PART // 2 * planes, slots) for j in chips]
        rows = jnp.concatenate(rows, axis=1)
        more = [jnp.dot(rows, second[n], preferred_element_type=jnp.float32) for n in range(2)]
        return dense + jnp.concatenate(more, axis=0)

    def finish(q):
        f, _ = place(q)
        for step in az_steps:
            az_copy(q, step).wait_recv()
        own_planes(q).wait()

        @pl.loop(0, PART // 2)
        def _(pair):
            first = (q % parts) * PART + pair * 2
            both = [planes_in[f, :, first + x].reshape(n_az * planes, block) for x in range(2)]
            found = jnp.dot(cas_ref[...], jnp.concatenate(both, axis=1), preferred_element_type=jnp.float32)
            found = found.astype(jnp.bfloat16)
            for x in range(2):
                for k in range(n_az):
                    spectra[f, k, first + x] = found[k * planes:(k + 1) * planes, x * block:(x + 1) * block]

        for step in az_steps:
            back_copy(q, step).start()
        own_spectra(q).start()

    def apply_radial(f):
        @pl.loop(0, parts)
        def _(part):
            for step in az_steps:
                back_copy(f * parts + part, step).wait_recv()
            own_spectra(f * parts + part).wait()

        @pl.when(f >= 2)
        def _():
            out_copy(f - 2).wait()

        @pl.loop(0, planes // 16)
        def _(part):
            here = pl.ds(pl.multiple_of(part * 16, 16), 16)
            takes_second = second_op_ref[here]
            both = [[], []]
            for b in range(n_az):
                by_mode = jnp.swapaxes(modes[f, b, :, here], 0, 1)
                later = by_mode * takes_second
                both[0].append((by_mode - later).reshape(16 * slab, block))
                both[1].append(later.reshape(16 * slab, block))
            rows = jnp.concatenate(both[0] + both[1], axis=1)
            mapped = jnp.dot(rows, turned_ops[...], preferred_element_type=jnp.float32)
            results[f % 2, here] = mapped.astype(jnp.bfloat16).reshape(16, slab, radial)

        out_copy(f).start()

    counts = [counts_ref[j] for j in range(n_rad)]
    starts = [0 * counts[0]]
    for j in range(1, n_rad):
        starts.append(starts[-1] + counts[j - 1])

    if paired:
        row, column = grids(slots, slots)
        low = slots // 2
        mine, theirs = counts_ref[rad], counts_ref[chip * 2 + 1 - core]
        for n, (count, offset) in enumerate([(mine, core * theirs), (theirs, (1 - core) * mine)]):
            spot, held = row + offset, row < count
            near[n * slots:(n + 1) * slots, :] = one_hot((spot == column) & held)
            rest[n * slots:(n + 1) * slots, :] = one_hot((spot == slots + column) & held & (column < low))
            rest[(n + 2) * slots:(n + 3) * slots, :] = one_hot((spot == low + column) & held & (column >= low))

    lay_out(0)
    pl.semaphore_wait(barrier, n_rad + n_az - 2)
    if paired:
        for q in range(AHEAD):
            pair_copy(q).start()

    @pl.loop(0, AHEAD)
    def _(q):
        start_rad(q)

    if paired:
        for q in range(AHEAD, parts):
            pair_copy(q).start()

    row, column = grids(slots, radial)
    if paired:
        for j in chips:
            begin, total, here = starts[2 * j], counts[2 * j] + counts[2 * j + 1], slice(j * slots, (j + 1) * slots)
            pack[here, :] = one_hot((row + begin == column) & (row < total))
            after = row + slots
            second[0, here, :] = one_hot((after + begin == column) & (after < total) & (row < low))
            after = row + low
            second[1, here, :] = one_hot((after + begin == column) & (after < total) & (row >= low))
    else:
        for j in range(n_rad):
            pack[j * slots:(j + 1) * slots, :] = one_hot((row + starts[j] == column) & (row < counts[j]))
    for n in range(2):
        turned_ops[n * radial:(n + 1) * radial, :] = ops_ref[n].T

    @pl.loop(0, chunks)
    def _(q):
        f, here = place(q)

        @pl.when((q % parts == 0) & (f + 1 < fields))
        def _():
            @pl.when(f + 2 < fields)
            def _():
                raw_copy(f + 2).start()

            lay_out(f + 1)
            if paired:
                for part in range(parts):
                    pair_copy(q + parts + part).start()

        @pl.when(q + AHEAD < chunks)
        def _():
            start_rad(q + AHEAD)

        for step in rad_steps:
            rad_copy(q, step).wait_recv()
        own_shells(q).wait()
        dense = dense_rows(q).astype(jnp.bfloat16)
        for k in range(n_az):
            packed[f, k, here] = dense[:, k * block:(k + 1) * block].reshape(PART, planes, block)

        for step in az_steps:
            az_copy(q, step).start()
        own_planes(q).start()

        @pl.when(q > 0)
        def _():
            finish(q - 1)

        @pl.when((q % parts == parts // 2) & (f > 0))
        def _():
            apply_radial(f - 1)

    finish(chunks - 1)
    apply_radial(fields - 1)

    @pl.loop(0, chunks)
    def _(q):
        if paired:
            pair_copy(q).wait_send()
        for step in rad_steps:
            rad_copy(q, step).wait_send()
        for step in az_steps:
            az_copy(q, step).wait_send()
            back_copy(q, step).wait_send()

    out_copy(fields - 2).wait()
    out_copy(fields - 1).wait()


def whole(field, shell_counts, cas_table, radial_ops, second_op, n_az, n_rad, paired):
    planes, fields, slots, length = field.shape
    slab = length // n_rad
    radial = radial_ops.shape[1]
    block = radial // n_az
    chunks = fields * slab // PART
    units = PART + PART // 2
    kind = field.dtype
    dma = pltpu.SemaphoreType.DMA
    spread = pltpu.VMEM((fields, n_az, slab, planes, block), kind)
    if paired:
        shells = pltpu.VMEM((n_rad // 2, chunks, units, planes, slots), kind)
        extra = [
            pltpu.VMEM((chunks, n_rad, PART, planes // 2, slots), kind),
            pltpu.VMEM((n_rad, chunks, units, planes // 2, slots), kind),
            pltpu.VMEM((2 * slots, slots), kind),
            pltpu.VMEM((4 * slots, slots), kind),
            pltpu.VMEM((2, n_rad // 2 * slots, radial), kind),
            dma((chunks,)), dma((chunks,)),
        ]
    else:
        shells = pltpu.VMEM((n_rad, fields, slab, planes, slots), kind)
        extra = []
    vmem = pl.BlockSpec(memory_space=pltpu.VMEM)
    return pl.pallas_call(
        functools.partial(whole_kernel, n_az, n_rad, paired),
        in_specs=[pl.BlockSpec(memory_space=pl.ANY), pl.BlockSpec(memory_space=pltpu.SMEM), vmem, vmem, vmem],
        out_specs=pl.BlockSpec(memory_space=pl.ANY),
        out_shape=jax.ShapeDtypeStruct((planes, fields, slab, radial), kind),
        scratch_shapes=[
            pltpu.VMEM((2, planes, slots, length), kind),
            pltpu.VMEM((n_rad, fields, slab, planes, slots), kind),
            shells, spread, spread, spread, spread,
            pltpu.VMEM((2, planes, slab, radial), kind),
            pltpu.VMEM((2 * radial, radial), kind),
            pltpu.VMEM((n_rad * slots // (2 if paired else 1), radial), kind),
            dma((chunks, n_rad)), dma((chunks, n_rad)),
            dma((chunks, n_az)), dma((chunks, n_az)),
            dma((chunks, n_az)), dma((chunks, n_az)),
            dma((chunks, 3)), dma((fields,)), dma((fields,)),
        ] + extra,
        compiler_params=pltpu.CompilerParams(
            collective_id=1 if paired else 0, has_side_effects=True, vmem_limit_bytes=VMEM_LIMIT),
    )(field, shell_counts, cas_table, radial_ops, second_op)


def hand_over_kernel(from_ref, to_ref):
    to_ref[...] = from_ref[...]


def hand_over(result):
    block = (result.shape[0] // 4,) + result.shape[1:]
    spec = pl.BlockSpec(block, lambda n: (n, 0, 0, 0))
    return pl.pallas_call(
        hand_over_kernel,
        grid=(4,),
        in_specs=[spec],
        out_specs=spec,
        out_shape=jax.ShapeDtypeStruct(result.shape, result.dtype),
        compiler_params=pltpu.CompilerParams(vmem_limit_bytes=VMEM_LIMIT),
    )(result)


def per_device(field, shell_counts, op_index, radial_ops):
    planes, fields, slots, cells = field.shape
    n_az, n_rad = lax.axis_size("az"), lax.axis_size("rad")
    comps_all = planes * n_az
    radial = radial_ops.shape[1]
    cas_table = make_table(comps_all)
    comp_ids = lax.axis_index("az") * planes + jnp.arange(planes, dtype=jnp.int32)
    mode_ids = jnp.minimum(comp_ids, comps_all - comp_ids)
    slab = cells // n_rad
    if fields < 2 or slots % 128 or cells % 128 or n_rad % 4 or slab % 16 or planes % 32 or radial % (128 * n_az):
        row_slot = slot_index(shell_counts, slots, radial)
        return plain_path(field, row_slot, cas_table, jnp.take(op_index, mode_ids), radial_ops)
    numbers = jnp.arange(op_index.shape[0], dtype=jnp.int32)
    chosen_ids = jnp.sum(jnp.where(mode_ids[:, None] == numbers[None, :], op_index[None, :], 0), axis=1)
    second_op = jnp.broadcast_to(chosen_ids[:, None, None], (planes, slab, radial // n_az)).astype(field.dtype)
    chips = jnp.arange(n_rad, dtype=jnp.int32) // 2
    together = jnp.sum(jnp.where(chips[:, None] == chips[None, :], shell_counts[None, :], 0), axis=1)
    operands = (field, shell_counts, cas_table, radial_ops, second_op)
    result = lax.cond(
        2 * jnp.max(together) <= 3 * slots,
        lambda *given: whole(*given, n_az, n_rad, True),
        lambda *given: whole(*given, n_az, n_rad, False),
        *operands)
    return hand_over(result)


def solution(mesh):
    return jax.shard_map(
        per_device,
        mesh=mesh,
        in_specs=(P("az", None, "rad", None), P(), P(), P()),
        out_specs=P("az", None, "rad", None),
        check_vma=False,
    )
```
